256 devices in a mesh: dp: 4 (over x), gx: 8 (over y, z_lo), gy: 8 (over z_hi, core).
Axes of the slice: x: 4, y: 4, z: 8 (z_hi: 4, z_lo: 2; z = z_hi * 2 + z_lo), core: 2. Of those that a mesh axis runs over, the one named last changes fastest.
Arguments:
- field: float32 [4, 32, 64, 128, 128], P('dp', None, 'gx', 'gy'), may hold values from -6 to 6
- cotangent: float32 [4, 32, 64, 128, 128], P('dp', None, 'gx', 'gy'), may hold values from -6 to 6
- spectral_weight: float32 [512, 32768], P(('gx', 'gy'), 'dp'), may hold values from -1 to 1
- pointwise_weight: float32 [32, 32], replicated, may hold values from -1 to 1
- bias: float32 [32], replicated, may hold values from -3 to 3
Outputs:
- grad_input: float32 [4, 32, 64, 128, 128], P('dp', None, 'gx', 'gy')
- grad_spectral: float32 [512, 32768], P(('gx', 'gy'), 'dp')
The draws below stay inside these ranges and needn't reach their ends.
All inputs are finite; a program needn't handle non-finite values.
Results may differ from the reference program's by a relative error of at most 0.00011.
Values sent between devices are 32-bit elements; how exact they have to be, the bound alone decides.
A program may use at most 128 MiB of HBM per device.

```python
import math
import jax
import jax.numpy as jnp
from jax import lax

C = 32
MX = 16
MY = 32
MZ = 16
NZ = 128
NX = 64
NY = 128
SAMPLES = 4


def shard_levels(key, shape, shards, least, high):
    level, own = 1.0, jax.random.fold_in(key, 6)
    for dim, parts in shards:
        steps = jnp.exp(jax.random.uniform(jax.random.fold_in(own, dim), (parts,), jnp.float32, least / len(shards), high / len(shards)))
        level = level * jnp.repeat(steps, shape[dim] // parts).reshape([-1 if axis == dim else 1 for axis in range(len(shape))])
    return level


def bell_draw(own_key, shape, spread, most, shards=(), kind=jnp.bfloat16):
    result = jax.random.normal(own_key, shape, jnp.float32) * spread
    if len(shards) > 0:
        result = shard_levels(own_key, shape, shards, -0.22, 0.18) * result
    return jnp.clip(result, min=-most, max=most).astype(kind)


def setup_inputs(seed: int = 0) -> dict:
    splits = jax.random.split(jax.random.key(seed), 6)
    field = bell_draw(splits[0], (SAMPLES, C, NX, NY, NZ), 1.0, 6.0, ((0, 4), (2, 8), (3, 8)), jnp.float32)
    cotangent = bell_draw(splits[1], (SAMPLES, C, NX, NY, NZ), 1.0, 6.0, ((0, 4), (2, 8), (3, 8)), jnp.float32)
    spectral_weight = bell_draw(splits[2], (MX * MY, MZ * C * C * 2), C ** -0.5, 1.0, ((0, 64), (1, 4)), jnp.float32)
    pointwise_weight = bell_draw(splits[3], (C, C), C ** -0.5, 1.0, (), jnp.float32)
    bias = bell_draw(splits[4], (C,), 0.5, 3.0, (), jnp.float32)
    return {"field": field, "cotangent": cotangent, "spectral_weight": spectral_weight, "pointwise_weight": pointwise_weight, "bias": bias}


exact_prec = lax.Precision.HIGHEST

def phases(count, freqs):
    positions = jnp.arange(count, dtype=jnp.int32)
    turns = jnp.mod(positions[:, None] * freqs[None, :], count)
    return turns.astype(jnp.float32) * (2.0 * math.pi / count)

def forward_pairs(count, freqs):
    theta = phases(count, freqs)
    cosine, sine = (jnp.cos(theta), jnp.sin(theta))
    return jnp.stack([jnp.stack([cosine, -sine], -1), jnp.stack([sine, cosine], -1)], -2)

def inverse_pairs(count, freqs):
    theta = phases(count, freqs)
    cosine, sine = (jnp.cos(theta), jnp.sin(theta))
    return jnp.stack([jnp.stack([cosine, sine], -1), jnp.stack([-sine, cosine], -1)], -2)

def depth_table(count, freqs):
    theta = phases(count, freqs)
    return jnp.stack([jnp.cos(theta), -jnp.sin(theta)], -1)

def gelu_slope(values):
    normal_cdf = 0.5 * (1.0 + lax.erf(values / math.sqrt(2.0)))
    return normal_cdf + values * jnp.exp(-0.5 * values * values) / math.sqrt(2.0 * math.pi)

def mix_modes(weight, spec):
    wreal, wimag = (weight[..., 0], weight[..., 1])
    sreal, simag = (spec[..., 0], spec[..., 1])
    form = 'abkoc,abkc->abko'
    yreal = jnp.einsum(form, wreal, sreal, precision=exact_prec) - jnp.einsum(form, wimag, simag, precision=exact_prec)
    yimag = jnp.einsum(form, wreal, simag, precision=exact_prec) + jnp.einsum(form, wimag, sreal, precision=exact_prec)
    return jnp.stack([yreal, yimag], -1)

def mix_adjoint(weight, spec):
    wreal, wimag = (weight[..., 0], weight[..., 1])
    zreal, zimag = (spec[..., 0], spec[..., 1])
    form = 'abkoc,abko->abkc'
    vreal = jnp.einsum(form, wreal, zreal, precision=exact_prec) + jnp.einsum(form, wimag, zimag, precision=exact_prec)
    vimag = jnp.einsum(form, wreal, zimag, precision=exact_prec) - jnp.einsum(form, wimag, zreal, precision=exact_prec)
    return jnp.stack([vreal, vimag], -1)

def outer_conj(spec_z, spec_u):
    zreal, zimag = (spec_z[..., 0], spec_z[..., 1])
    ureal, uimag = (spec_u[..., 0], spec_u[..., 1])
    form = 'abko,abkc->abkoc'
    greal = jnp.einsum(form, zreal, ureal, precision=exact_prec) + jnp.einsum(form, zimag, uimag, precision=exact_prec)
    gimag = jnp.einsum(form, zimag, ureal, precision=exact_prec) - jnp.einsum(form, zreal, uimag, precision=exact_prec)
    return jnp.stack([greal, gimag], -1)

def reference(field, cotangent, spectral_weight, pointwise_weight, bias):
    freq_x = jnp.arange(MX, dtype=jnp.int32) - MX // 2
    freq_y = jnp.arange(MY, dtype=jnp.int32) - MY // 2
    freq_z = jnp.arange(MZ, dtype=jnp.int32)
    fwd_x, fwd_y = (forward_pairs(NX, freq_x), forward_pairs(NY, freq_y))
    inv_x, inv_y = (inverse_pairs(NX, freq_x), inverse_pairs(NY, freq_y))
    ztable = depth_table(NZ, freq_z)
    weight = spectral_weight.reshape(MX, MY, MZ, C, C, 2)
    scale_cells = 1.0 / math.sqrt(NX * NY * NZ)
    scale_modes = 1.0 / math.sqrt(MX * MY * MZ)

    def transform(grid):
        section_z = jnp.einsum('cxyz,zkr->xykcr', grid, ztable, precision=exact_prec)
        section_y = jnp.einsum('xykcr,yjrq->xjkcq', section_z, fwd_y, precision=exact_prec)
        return jnp.einsum('xjkcq,xiqt->ijkct', section_y, fwd_x, precision=exact_prec)

    def untransform(spec):
        section_x = jnp.einsum('ijkct,xitq->xjkcq', spec, inv_x, precision=exact_prec)
        section_y = jnp.einsum('xjkcq,yjqr->xykcr', section_x, inv_y, precision=exact_prec)
        return jnp.einsum('xykcr,zkr->cxyz', section_y, ztable, precision=exact_prec)

    def one_sample(carry, pair):
        grid, grad_out = pair
        spec_u = transform(grid) * scale_cells
        spec_y = mix_modes(weight, spec_u)
        conv = untransform(spec_y) * scale_modes
        local = jnp.einsum('oc,cxyz->oxyz', pointwise_weight, grid, precision=exact_prec)
        pre = conv + local + bias[:, None, None, None]
        slope_grad = grad_out * gelu_slope(pre)
        spec_z = transform(slope_grad) * scale_modes
        carry = carry + outer_conj(spec_z, spec_u)
        spec_v = mix_adjoint(weight, spec_z)
        grad_local = jnp.einsum('oc,oxyz->cxyz', pointwise_weight, slope_grad, precision=exact_prec)
        return (carry, grad_local + untransform(spec_v) * scale_cells)
    start = jnp.zeros((MX, MY, MZ, C, C, 2), jnp.float32)
    total, grad_input = lax.scan(one_sample, start, (field, cotangent))
    return (grad_input, total.reshape(MX * MY, MZ * C * C * 2))
```

```python
import math

import jax
import jax.numpy as jnp
import numpy as np
from jax import lax
from jax.experimental import pallas as pl
from jax.experimental.pallas import tpu as pltpu
from jax.sharding import PartitionSpec as P

C = 32
MX = 16
MY = 32
MZ = 16
NX = 64
NY = 128
NZ = 128

F32 = jnp.float32
BF16 = jnp.bfloat16
MESH = pl.DeviceIdType.MESH

KX = np.array([4 * ((d // 2) % 4) + 2 * (d % 2) + d // 8 for d in range(16)])


def cos_sin(count, freqs):
    turns = np.mod(np.arange(count)[:, None] * freqs[None, :], count)
    theta = turns * (2.0 * math.pi / count)
    return np.cos(theta), np.sin(theta)


def halves(table):
    table = table.astype(np.float32)
    high = table.astype(jnp.bfloat16)
    low = (table - high.astype(np.float32)).astype(jnp.bfloat16)
    return [high, low]


def tables():
    eye8 = np.eye(8)
    cz, sz = cos_sin(NZ, np.arange(MZ))
    ztable = np.stack([cz, -sz], -1)
    cx, sx = cos_sin(NX, KX - MX // 2)
    cy, sy = cos_sin(NY, np.arange(MY) - MY // 2)

    def forward(c, s):
        return np.stack([np.stack([c, -s], -1), np.stack([s, c], -1)], -2)

    def inverse(c, s):
        return np.stack([np.stack([c, s], -1), np.stack([-s, c], -1)], -2)

    z_fwd = np.einsum("zkr,cd->czrkd", ztable, eye8).reshape(8 * NZ, 2 * MZ * 8)
    z_inv = np.ascontiguousarray(z_fwd.T)
    fx = forward(cx, sx).reshape(8, 8, 16, 2, 2)
    x_fwd = np.einsum("gxdrq,yw->dqygrxw", fx, eye8).reshape(256, 1024)
    ix = inverse(cx, sx).reshape(8, 8, 16, 2, 2)
    x_inv = np.einsum("gxdqr,yw->grxydqw", ix, eye8).reshape(1024, 256)
    fy = forward(cy, sy).reshape(16, 8, MY, 2, 2)
    y_fwd = np.einsum("dyjqp->pjdqy", fy).reshape(64, 256)
    iy = inverse(cy, sy).reshape(16, 8, MY, 2, 2)
    y_inv = np.einsum("dyjpr->drypj", iy).reshape(256, 64)

    use = np.zeros((128, 2, 2, C, 2), np.float32)
    for i in range(C):
        use[i, 0, :, i, 0] = 1.0
        use[C + i, 0, :, i, 1] = -1.0
        use[C + i, 1, :, i, 0] = 1.0
        use[i, 1, :, i, 1] = 1.0
    spread = np.zeros((128, 16, 2, 2, C, 2), np.float32)
    for b in range(2):
        for o in range(C):
            spread[b * C + o, o // 2, b, o % 2] = 1.0
    spread = spread.reshape(128, 4096)
    fold = np.zeros((2, 2, C, 2, 128), np.float32)
    for i in range(C):
        fold[0, :, i, 0, i] = 1.0
        fold[1, :, i, 1, i] = 1.0
        fold[1, :, i, 0, C + i] = 1.0
        fold[0, :, i, 1, C + i] = -1.0
    rows8 = np.repeat(np.eye(C), 8, axis=0)
    out = []
    for t in (z_fwd, x_fwd, y_fwd, y_inv, x_inv, z_inv):
        out += halves(t)
    out += [
        t.astype(jnp.bfloat16)
        for t in (
            use.reshape(128, 256),
            spread,
            np.ascontiguousarray(spread.T),
            fold.reshape(256, 128),
            rows8,
        )
    ]
    return out


TABLES = tables()


def gelu_slope(values):
    normal_cdf = 0.5 * (1.0 + lax.erf(values * math.sqrt(0.5)))
    return normal_cdf + values * jnp.exp(-0.5 * values * values) * (1.0 / math.sqrt(2.0 * math.pi))


def split(x):
    high = x.astype(BF16)
    return high, (x - high.astype(F32)).astype(BF16)


def dot(a, b):
    return jnp.dot(a, b, preferred_element_type=F32)


def left3(high, low, x):
    xh, xl = split(x)
    return dot(high, xh) + (dot(low, xh) + dot(high, xl))


def right3(x, high, low):
    xh, xl = split(x)
    return dot(xh, high) + (dot(xl, high) + dot(xh, low))


def right2(x, table):
    xh, xl = split(x)
    return dot(xh, table) + dot(xl, table)


def lanes_of(rows):
    return lax.broadcasted_iota(jnp.int32, (rows, 128), 1)


def roll(x, shift):
    shift = shift % 128
    return pltpu.roll(x, shift, axis=1) if shift else x


def swap_groups(blocks):
    lane = lanes_of(32)
    out = []
    for a in range(4):
        total = jnp.zeros((32, 128), F32)
        for b in range(4):
            keep = ((lane % 32) // 8 == b) & (lane < 64)
            total = total + jnp.where(keep, roll(blocks[b], (b - a) * 8), 0.0)
        out.append(total)
    return out


def pack_kz(v):
    lane = lanes_of(32)
    return [
        jnp.where(lane < 32, roll(v[:32], -kzg * 32), roll(v[32:], 32 - kzg * 32)) for kzg in range(4)
    ]


def unpack_kz(blocks):
    lane = lanes_of(32)
    parts = []
    for p in range(2):
        total = jnp.zeros((32, 128), F32)
        for kzg in range(4):
            total = total + jnp.where(lane // 32 == kzg, roll(blocks[kzg], (kzg - p) * 32), 0.0)
        parts.append(total)
    return jnp.concatenate(parts, axis=0)


def kernel(
    field_hbm,
    cot_hbm,
    weight_hbm,
    point_ref,
    bias_ref,
    *rest,
):
    n_tab = len(TABLES)
    tab_hbm = rest[:n_tab]
    gi_hbm, gs_hbm = rest[n_tab : n_tab + 2]
    scratch = rest[n_tab + 2 :]
    tab = scratch[:n_tab]
    (
        field,
        cot,
        weight,
        local,
        slope,
        grad,
        gspec,
        point_kron,
        use_ref,
        out1,
        recv1,
        out2,
        recv2,
        out3,
        recv3,
        out4,
        recv4,
        out5,
        recv5,
        out6,
        recv6,
        in_sem,
        tab_sem,
        done_sem,
        send_sem,
        recv_sem,
    ) = scratch[n_tab:]
    (zfh, zfl, xfh, xfl, yfh, yfl, yih, yil, xih, xil, zih, zil, use, spread, gather, fold, rows8) = tab

    s = lax.axis_index("dp")
    gx = lax.axis_index("gx")
    h = lax.axis_index("gy")
    yp = gx // 2
    zl = gx % 2
    place = 2 * h + zl
    scale_cells = 1.0 / math.sqrt(NX * NY * NZ)
    scale_modes = 1.0 / math.sqrt(MX * MY * MZ)

    def fetch(k):
        return pltpu.make_async_copy(tab_hbm[k], tab[k], tab_sem.at[k])

    inputs = [
        pltpu.make_async_copy(a, b, in_sem.at[k])
        for k, (a, b) in enumerate(((field_hbm, field), (weight_hbm, weight), (cot_hbm, cot)))
    ]
    fetch(0).start()
    fetch(1).start()
    inputs[0].start()
    for k in range(2, n_tab):
        fetch(k).start()
    inputs[1].start()
    inputs[2].start()

    def push(src, dst, stage, device):
        pltpu.make_async_remote_copy(
            src_ref=src,
            dst_ref=dst,
            send_sem=send_sem.at[stage],
            recv_sem=recv_sem.at[stage],
            device_id=device,
            device_id_type=MESH,
        ).start()

    def keep(src, dst, stage):
        pltpu.make_async_copy(src, dst, recv_sem.at[stage]).start()

    def arrived(buffer, stage):
        pltpu.make_async_copy(buffer, buffer, recv_sem.at[stage]).wait()

    def sent(buffer, stage):
        pltpu.make_async_copy(buffer, buffer, send_sem.at[stage]).wait()

    def over_gx(src, dst, stage, k):
        to = (gx + k) % 8
        push(src.at[to], dst.at[gx], stage, (s, to, h))

    def over_ring(src, dst, stage):
        def one(k, carry):
            to = (place + k) % 16
            push(src.at[to], dst.at[place], stage, (s, 2 * yp + to % 2, to // 2))
            return carry

        lax.fori_loop(1, 16, one, 0)
        keep(src.at[place], dst.at[place], stage)

    on_self = yp == h % 4

    def to_owner(src, dst, stage):
        first = s * 4 + h % 4

        def one(k, carry):
            to = (first + k) % 16
            push(src.at[to], dst.at[s * 4 + yp], stage, (to // 4, 2 * (h % 4) + zl, (h // 4) * 4 + to % 4))
            return carry

        lax.fori_loop(1, 16, one, 0)
        pl.when(on_self)(lambda: keep(src.at[first], dst.at[s * 4 + yp], stage))

        @pl.when(jnp.logical_not(on_self))
        def _():
            one(0, 0)

    def from_owner(src, dst, stage):
        first = s * 4 + yp

        def one(k, carry):
            to = (first + k) % 16
            push(src.at[to], dst.at[s * 4 + h % 4], stage, (to // 4, 2 * (to % 4) + zl, (h // 4) * 4 + yp))
            return carry

        lax.fori_loop(1, 16, one, 0)
        pl.when(on_self)(lambda: keep(src.at[first], dst.at[s * 4 + h % 4], stage))

        @pl.when(jnp.logical_not(on_self))
        def _():
            one(0, 0)

    def depth_forward(grid, cg, dst):
        total = jnp.zeros((128, 256), F32)
        for pair in range(4):
            block = jnp.concatenate(
                [grid[cg * 8 + pair * 2 + k].reshape(128, 128) for k in range(2)], axis=1
            )
            rows = pl.ds(pair * 256, 256)
            total = total + right3(block, zfh[rows], zfl[rows])
        total = total.reshape(8, 2, 8, 256)
        for yh in range(2):
            for r in range(2):
                dst[cg * 2 + yh, r] = total[:, yh, :, r * 128 : (r + 1) * 128]

    def send_group(src, dst, stage, k):
        cg = (yp + k) % 4
        if k == 0:
            other = gx + 1 - 2 * zl
            push(src.at[other], dst.at[gx], stage, (s, other, h))
            keep(src.at[gx], dst.at[gx], stage)
        else:
            for yh in range(2):
                to = 2 * cg + (zl + yh) % 2
                push(src.at[to], dst.at[gx], stage, (s, to, h))

    def x_forward(buf):
        return left3(xfh[...], xfl[...], buf[...].reshape(1024, 128))

    def middle_forward(first, scale):
        n = 0 if first else 1
        arrived(recv1.at[n], 6 * n)
        out2[n] = x_forward(recv1.at[n]).reshape(16, 16, 128)
        over_ring(out2.at[n], recv2.at[n], 6 * n + 1)
        arrived(recv2.at[n], 6 * n + 1)
        v = left3(yfh[...], yfl[...], recv2[n].reshape(256, 128)) * scale
        for kzg, block in enumerate(pack_kz(v)):
            out3[n, pl.ds(kzg * 4, 4)] = block.reshape(4, 8, 128)
        to_owner(out3.at[n], recv3.at[n], 6 * n + 2)

    def owner_rows(n):
        arrived(recv3.at[n], 6 * n + 2)
        value = recv3[n].reshape(4, 4, 8, 128)
        return jnp.concatenate(swap_groups([value[:, cg].reshape(32, 128) for cg in range(4)]), axis=0)

    def middle_inverse(rows, n, scale):
        blocks = swap_groups([rows[kz * 32 : (kz + 1) * 32] * scale for kz in range(4)])
        for cg in range(4):
            block = blocks[cg].reshape(4, 8, 128)
            for t in range(4):
                out4[n, t * 4 + cg] = block[t]
        from_owner(out4.at[n], recv4.at[n], 6 * n + 3)
        arrived(recv4.at[n], 6 * n + 3)
        value = recv4[n].reshape(4, 32, 128)
        planes = unpack_kz([value[kzg] for kzg in range(4)])
        out5[n] = left3(yih[...], yil[...], planes).reshape(16, 16, 128)
        over_ring(out5.at[n], recv5.at[n], 6 * n + 4)
        arrived(recv5.at[n], 6 * n + 4)
        rows5 = recv5[n].reshape(256, 128)
        high, low = split(rows5)
        for k in range(8):
            part = pl.ds(k * 128, 128)
            block = dot(xih[part], high) + (dot(xil[part], high) + dot(xih[part], low))
            out6[n, k] = block.reshape(2, 8, 8, 128)
        for k in range(1, 8):
            over_gx(out6.at[n], recv6.at[n], 6 * n + 5, k)
        keep(out6.at[n, gx], recv6.at[n, gx], 6 * n + 5)

    def depth_inverse(n, cg, finish):
        halves_ = []
        for yh in range(2):
            halves_.append(
                jnp.concatenate([recv6[n, cg * 2 + yh, r].reshape(64, 128) for r in range(2)], axis=1)
            )
        high, low = split(jnp.concatenate(halves_, axis=0))
        for pair in range(4):
            cols = pl.ds(pair * 256, 256)
            value = dot(high, zih[:, cols]) + (dot(low, zih[:, cols]) + dot(high, zil[:, cols]))
            for k in range(2):
                for yh in range(2):
                    finish(
                        cg * 8 + pair * 2 + k,
                        yh,
                        value[yh * 64 : (yh + 1) * 64, k * 128 : (k + 1) * 128].reshape(8, 8, 128),
                    )

    def kron(transposed):
        same = lax.broadcasted_iota(jnp.int32, (256, 256), 0) % 8 == (
            lax.broadcasted_iota(jnp.int32, (256, 256), 1) % 8
        )
        dims = (((1,), (1 if transposed else 0,)), ((), ()))
        for k, half in enumerate(split(point_ref[...])):
            tall = lax.dot_general(rows8[...], half, dims, preferred_element_type=F32).astype(BF16)
            wide = lax.dot_general(
                tall, rows8[...], (((1,), (1,)), ((), ())), preferred_element_type=F32
            )
            point_kron[k] = jnp.where(same, wide, 0.0).astype(BF16)

    def pointwise(src, dst):
        def one(x, carry):
            block = jnp.concatenate([src[:, x, yh].reshape(256, 128) for yh in range(2)], axis=1)
            value = left3(point_kron[0], point_kron[1], block)
            for yh in range(2):
                dst[:, x, yh] = value[:, yh * 128 : (yh + 1) * 128].reshape(32, 8, 128)
            return carry

        lax.fori_loop(0, 8, one, 0)

    fetch(0).wait()
    fetch(1).wait()
    inputs[0].wait()
    for k in (1, 2, 3, 0):
        depth_forward(field, (yp + k) % 4, out1.at[0])
        send_group(out1.at[0], recv1.at[0], 0, k)
    for k in range(2, n_tab):
        fetch(k).wait()
    kron(False)
    pointwise(field, local)
    middle_forward(True, scale_cells)

    inputs[1].wait()
    operands = right2(owner_rows(0), use[...])
    for b in range(2):
        use_ref[b] = operands[:, b * 128 : (b + 1) * 128].reshape(4, 4, 8, 128)

    def mix(pair, total):
        both = []
        for b in range(2):
            products = []
            for kz in range(4):
                cols = pl.ds(pl.multiple_of((kz * 16 + pair) * 128, 128), 128)
                products.append((use_ref[b, kz] * weight[:, cols][None]).reshape(32, 128))
            both.append(jnp.concatenate(products, axis=0))
        rows = pl.ds(pl.multiple_of(pair * 256, 256), 256)
        return total + right2(jnp.concatenate(both, axis=1), gather[rows])

    mixed = lax.fori_loop(0, 16, mix, jnp.zeros((128, 128), F32))
    middle_inverse(mixed, 0, scale_modes)

    inputs[2].wait()
    arrived(recv6.at[0], 5)

    def slope_of(c, yh, value):
        pre = value + local[c, :, yh] + bias_ref[c]
        slope[c, :, yh] = cot[c, :, yh] * gelu_slope(pre)

    for k in (1, 2, 3, 0):
        cg = (yp + k) % 4
        depth_inverse(0, cg, slope_of)
        depth_forward(slope, cg, out1.at[1])
        send_group(out1.at[1], recv1.at[1], 6, k)
    kron(True)
    pointwise(slope, local)
    middle_forward(False, scale_modes)

    spectra = owner_rows(1)
    spec_high, spec_low = split(spectra)

    def adjoint(pair, carry):
        first, second = carry
        cols = pl.ds(pl.multiple_of(pair * 256, 256), 256)
        wide = dot(spec_high, spread[:, cols]) + dot(spec_low, spread[:, cols])
        zr = wide[:, :128].reshape(4, 4, 8, 128)
        zi = wide[:, 128:].reshape(4, 4, 8, 128)
        ones, twos = [], []
        for kz in range(4):
            cols = pl.ds(pl.multiple_of((kz * 16 + pair) * 128, 128), 128)
            tile = weight[:, cols][None]
            ones.append(zr[kz] * tile)
            twos.append(zi[kz] * tile)
            gspec[:, cols] = jnp.sum(zr[kz] * use_ref[0, kz] + zi[kz] * use_ref[1, kz], axis=0)
        return first + jnp.stack(ones), second + jnp.stack(twos)

    zero = jnp.zeros((4, 4, 8, 128), F32)
    first, second = lax.fori_loop(0, 16, adjoint, (zero, zero))
    both = jnp.concatenate([first.reshape(128, 128), second.reshape(128, 128)], axis=1)
    spec_out = pltpu.make_async_copy(gspec, gs_hbm, done_sem.at[4])
    spec_out.start()
    middle_inverse(right2(both, fold[...]), 1, scale_cells)
    arrived(recv6.at[1], 11)

    def finish(c, yh, value):
        grad[c, :, yh] = value + local[c, :, yh]

    results = []
    for cg in range(4):
        depth_inverse(1, cg, finish)
        part = pl.ds(cg * 8, 8)
        results.append(pltpu.make_async_copy(grad.at[part], gi_hbm.at[part], done_sem.at[cg]))
        results[-1].start()

    for n in range(2):
        sent(out1.at[n, pl.ds(0, 7)], 6 * n)
        sent(out2.at[n, pl.ds(0, 15)], 6 * n + 1)
        sent(out5.at[n, pl.ds(0, 15)], 6 * n + 4)
        sent(out6.at[n, pl.ds(0, 7)], 6 * n + 5)
        for buf, stage in ((out3, 6 * n + 2), (out4, 6 * n + 3)):
            sent(buf.at[n, pl.ds(0, 15)], stage)
            pl.when(jnp.logical_not(on_self))(lambda buf=buf, stage=stage: sent(buf.at[n, 0], stage))
    spec_out.wait()
    for copy in results:
        copy.wait()


def body(field, cotangent, spectral_weight, pointwise_weight, bias):
    shape = (C, 8, 2, 8, NZ)
    big = (2, 8, 2, 8, 8, 128)
    ring = (2, 16, 16, 128)
    modes = (2, 16, 8, 128)
    any_spec = pl.BlockSpec(memory_space=pl.ANY)
    grad_input, grad_spectral = pl.pallas_call(
        kernel,
        out_shape=(
            jax.ShapeDtypeStruct(shape, F32),
            jax.ShapeDtypeStruct(spectral_weight.shape, F32),
        ),
        in_specs=[any_spec] * 3
        + [pl.BlockSpec(memory_space=pltpu.VMEM), pl.BlockSpec(memory_space=pltpu.SMEM)]
        + [any_spec] * len(TABLES),
        out_specs=(any_spec, any_spec),
        scratch_shapes=[pltpu.VMEM(t.shape, BF16) for t in TABLES]
        + [
            pltpu.VMEM(shape, F32),
            pltpu.VMEM(shape, F32),
            pltpu.VMEM((8, 8192), F32),
            pltpu.VMEM(shape, F32),
            pltpu.VMEM(shape, F32),
            pltpu.VMEM(shape, F32),
            pltpu.VMEM((8, 8192), F32),
            pltpu.VMEM((2, 256, 256), BF16),
            pltpu.VMEM((2, 4, 4, 8, 128), F32),
            pltpu.VMEM(big, F32),
            pltpu.VMEM(big, F32),
            pltpu.VMEM(ring, F32),
            pltpu.VMEM(ring, F32),
            pltpu.VMEM(modes, F32),
            pltpu.VMEM(modes, F32),
            pltpu.VMEM(modes, F32),
            pltpu.VMEM(modes, F32),
            pltpu.VMEM(ring, F32),
            pltpu.VMEM(ring, F32),
            pltpu.VMEM(big, F32),
            pltpu.VMEM(big, F32),
            pltpu.SemaphoreType.DMA((3,)),
            pltpu.SemaphoreType.DMA((len(TABLES),)),
            pltpu.SemaphoreType.DMA((5,)),
            pltpu.SemaphoreType.DMA((12,)),
            pltpu.SemaphoreType.DMA((12,)),
        ],
        compiler_params=pltpu.CompilerParams(
            has_side_effects=True, vmem_limit_bytes=48 * 1024 * 1024
        ),
        name="fno_backward",
    )(
        field.reshape(shape),
        cotangent.reshape(shape),
        spectral_weight,
        pointwise_weight,
        bias,
        *[jnp.asarray(t) for t in TABLES],
    )
    return grad_input.reshape(field.shape), grad_spectral


def solution(mesh):
    placed = (
        P("dp", None, "gx", "gy", None),
        P("dp", None, "gx", "gy", None),
        P(("gx", "gy"), "dp"),
        P(),
        P(),
    )
    return jax.shard_map(
        body,
        mesh=mesh,
        in_specs=placed,
        out_specs=(P("dp", None, "gx", "gy", None), P(("gx", "gy"), "dp")),
        check_vma=False,
    )
```

```python
import math

import jax
import jax.numpy as jnp
import numpy as np
from jax import lax
from jax.experimental import pallas as pl
from jax.experimental.pallas import tpu as pltpu
from jax.sharding import PartitionSpec as P

C = 32
MX = 16
MY = 32
MZ = 16
NX = 64
NY = 128
NZ = 128

F32 = jnp.float32
BF16 = jnp.bfloat16
MESH = pl.DeviceIdType.MESH

KX = np.array([4 * ((d // 2) % 4) + 2 * (d % 2) + d // 8 for d in range(16)])


def cos_sin(count, freqs):
    turns = np.mod(np.arange(count)[:, None] * freqs[None, :], count)
    theta = turns * (2.0 * math.pi / count)
    return np.cos(theta), np.sin(theta)


def halves(table):
    table = table.astype(np.float32)
    high = table.astype(jnp.bfloat16)
    low = (table - high.astype(np.float32)).astype(jnp.bfloat16)
    return [high, low]


def tables():
    eye8 = np.eye(8)
    cz, sz = cos_sin(NZ, np.arange(MZ))
    ztable = np.stack([cz, -sz], -1)
    cx, sx = cos_sin(NX, KX - MX // 2)
    cy, sy = cos_sin(NY, np.arange(MY) - MY // 2)

    def forward(c, s):
        return np.stack([np.stack([c, -s], -1), np.stack([s, c], -1)], -2)

    def inverse(c, s):
        return np.stack([np.stack([c, s], -1), np.stack([-s, c], -1)], -2)

    z_fwd = np.einsum("zkr,cd->czrkd", ztable, eye8).reshape(8 * NZ, 2 * MZ * 8)
    z_inv = np.ascontiguousarray(z_fwd.T)
    fx = forward(cx, sx).reshape(8, 8, 16, 2, 2)
    fx = fx.reshape(4, 2, 8, 16, 2, 2)
    x_fwd = np.einsum("gzxdrq,yw->zdqygrxw", fx, eye8).reshape(2, 256, 512)
    ix = inverse(cx, sx).reshape(8, 8, 16, 2, 2)
    ix = ix.reshape(4, 2, 8, 16, 2, 2)
    x_inv = np.einsum("gzxdqr,yw->zgrxydqw", ix, eye8).reshape(8, 128, 256)
    fy = forward(cy, sy).reshape(16, 8, MY, 2, 2)
    y_fwd = np.einsum("dyjqp->pjdqy", fy).reshape(64, 256)
    iy = inverse(cy, sy).reshape(16, 8, MY, 2, 2)
    y_inv = np.einsum("dyjpr->drypj", iy).reshape(256, 64)

    use = np.zeros((128, 2, 2, C, 2), np.float32)
    for i in range(C):
        use[i, 0, :, i, 0] = 1.0
        use[C + i, 0, :, i, 1] = -1.0
        use[C + i, 1, :, i, 0] = 1.0
        use[i, 1, :, i, 1] = 1.0
    spread = np.zeros((128, 16, 2, 2, C, 2), np.float32)
    for b in range(2):
        for o in range(C):
            spread[b * C + o, o // 2, b, o % 2] = 1.0
    spread = spread.reshape(128, 4096)
    fold = np.zeros((2, 2, C, 2, 128), np.float32)
    for i in range(C):
        fold[0, :, i, 0, i] = 1.0
        fold[1, :, i, 1, i] = 1.0
        fold[1, :, i, 0, C + i] = 1.0
        fold[0, :, i, 1, C + i] = -1.0
    rows8 = np.repeat(np.eye(C), 8, axis=0)
    out = []
    for t in (z_fwd, x_fwd, y_fwd, y_inv, x_inv, z_inv):
        out += halves(t)
    out += [
        t.astype(jnp.bfloat16)
        for t in (
            use.reshape(128, 256),
            spread,
            np.ascontiguousarray(spread.T),
            fold.reshape(256, 128),
            rows8,
        )
    ]
    return out


TABLES = tables()


def gelu_slope(values):
    normal_cdf = 0.5 * (1.0 + lax.erf(values * math.sqrt(0.5)))
    return normal_cdf + values * jnp.exp(-0.5 * values * values) * (1.0 / math.sqrt(2.0 * math.pi))


def split(x):
    high = x.astype(BF16)
    return high, (x - high.astype(F32)).astype(BF16)


def dot(a, b):
    return jnp.dot(a, b, preferred_element_type=F32)


def left3(high, low, x):
    xh, xl = split(x)
    return dot(high, xh) + (dot(low, xh) + dot(high, xl))


def right3(x, high, low):
    xh, xl = split(x)
    return dot(xh, high) + (dot(xl, high) + dot(xh, low))


def right2(x, table):
    xh, xl = split(x)
    return dot(xh, table) + dot(xl, table)


def lanes_of(rows):
    return lax.broadcasted_iota(jnp.int32, (rows, 128), 1)


def roll(x, shift):
    shift = shift % 128
    return pltpu.roll(x, shift, axis=1) if shift else x


def swap_groups(blocks):
    group = (lanes_of(64) % 32) // 8
    out = []
    for a in range(4):
        total = blocks[a]
        for b in range(4):
            if b != a:
                total = jnp.where(group == b, roll(blocks[b], (b - a) * 8), total)
        out.append(total)
    return out


def pack_kz(v):
    lane = lanes_of(32)
    return [
        jnp.where(lane < 32, roll(v[:32], -j * 32), roll(v[32:], 32 - j * 32)) for j in range(4)
    ]


def unpack_kz(blocks):
    lane = lanes_of(32)
    parts = []
    for p in range(2):
        total = jnp.zeros((32, 128), F32)
        for j in range(4):
            total = total + jnp.where(lane // 32 == j, roll(blocks[j], (j - p) * 32), 0.0)
        parts.append(total)
    return jnp.concatenate(parts, axis=0)


def kernel(
    field_hbm,
    cot_hbm,
    weight_hbm,
    point_ref,
    bias_ref,
    *rest,
):
    n_tab = len(TABLES)
    tab_hbm = rest[:n_tab]
    gi_hbm, gs_hbm = rest[n_tab : n_tab + 2]
    scratch = rest[n_tab + 2 :]
    tab = scratch[:n_tab]
    (
        field,
        cot,
        weight,
        local,
        slope,
        grad,
        gspec,
        wloc,
        gloc,
        grecv,
        gsum,
        point_kron,
        use_ref,
        out1,
        recv1,
        out2,
        recv2,
        out5,
        recv5,
        out6,
        recv6,
        in_sem,
        tab_sem,
        done_sem,
        send_sem,
        recv_sem,
    ) = scratch[n_tab:]
    (zfh, zfl, xfh, xfl, yfh, yfl, yih, yil, xih, xil, zih, zil, use, spread, gather, fold, rows8) = tab

    s = lax.axis_index("dp")
    gx = lax.axis_index("gx")
    h = lax.axis_index("gy")
    yp = gx // 2
    zl = gx % 2
    place = 2 * h + zl
    on_self = yp == h % 4
    scale_cells = 1.0 / math.sqrt(NX * NY * NZ)
    scale_modes = 1.0 / math.sqrt(MX * MY * MZ)

    def mover(k):
        return (s, 2 * k + zl, (h // 4) * 4 + yp)

    def owner(k):
        return (s, 2 * (h % 4) + zl, (h // 4) * 4 + k)

    barrier = pltpu.get_barrier_semaphore()

    def hello(device):
        pl.semaphore_signal(barrier, inc=1, device_id=device, device_id_type=MESH)

    for k in range(1, 16):
        to = (place + k) % 16
        hello((s, 2 * yp + to % 2, to // 2))
    for k in range(1, 8):
        hello((s, (gx + k) % 8, h))
    for k in range(1, 4):
        hello(((s + k) % 4, gx, h))
        hello(mover((yp + k) % 4))
        hello(owner((h + k) % 4))

    @pl.when(jnp.logical_not(on_self))
    def _():
        hello(mover(yp))
        hello(owner(h % 4))

    def fetch(k):
        return pltpu.make_async_copy(tab_hbm[k], tab[k], tab_sem.at[k])

    inputs = [
        pltpu.make_async_copy(a, b, in_sem.at[k])
        for k, (a, b) in enumerate(((field_hbm, field), (weight_hbm, weight), (cot_hbm, cot)))
    ]
    fetch(0).start()
    fetch(1).start()
    inputs[0].start()
    inputs[1].start()
    for k in range(2, n_tab):
        fetch(k).start()
    inputs[2].start()

    def push(src, dst, out_sem, in_sem, device):
        pltpu.make_async_remote_copy(
            src_ref=src,
            dst_ref=dst,
            send_sem=send_sem.at[out_sem],
            recv_sem=recv_sem.at[in_sem],
            device_id=device,
            device_id_type=MESH,
        ).start()

    def keep(src, dst, in_sem):
        pltpu.make_async_copy(src, dst, recv_sem.at[in_sem]).start()

    def arrived(buffer, in_sem):
        pltpu.make_async_copy(buffer, buffer, recv_sem.at[in_sem]).wait()

    def sent(buffer, out_sem):
        pltpu.make_async_copy(buffer, buffer, send_sem.at[out_sem]).wait()

    def send_gx(src, dst, stage, to_zl, dy):
        to_yp = (yp + dy) % 4
        block = to_zl * 4 + to_yp
        push(src.at[block], dst.at[zl * 4 + yp], stage, stage + zl, (s, 2 * to_yp + to_zl, h))

    def keep_gx(src, dst, stage):
        block = zl * 4 + yp
        keep(src.at[block], dst.at[block], stage + zl)

    def over_ring(src, dst, stage):
        for k in (8, 7, 9, 6, 10, 5, 11, 4, 12, 3, 13, 2, 14, 1, 15):
            to = (place + k) % 16
            push(src.at[to], dst.at[place], stage, stage, (s, 2 * yp + to % 2, to // 2))
        keep(src.at[place], dst.at[place], stage)

    def depth_forward(grid, half, dst):
        total = jnp.zeros((256, 256), F32)
        for pair in range(4):
            block = jnp.concatenate(
                [
                    jnp.concatenate(
                        [grid[cg * 8 + pair * 2 + k, :, half].reshape(64, 128) for k in range(2)], axis=1
                    )
                    for cg in range(4)
                ],
                axis=0,
            )
            rows = pl.ds(pair * 256, 256)
            total = total + right3(block, zfh[rows], zfl[rows])
        for r in range(2):
            blocks = [total[cg * 64 : (cg + 1) * 64, r * 128 : (r + 1) * 128] for cg in range(4)]
            for k, block in enumerate(swap_groups(blocks)):
                dst[half * 4 + k, r] = block.reshape(8, 8, 128)

    def send_half(n, half_is_own):
        half = zl if half_is_own else 1 - zl
        for dy in (2, 1, 3):
            send_gx(out1.at[n], recv1.at[n], 6 * n, half, dy)
        if half_is_own:
            keep_gx(out1.at[n], recv1.at[n], 6 * n)
        else:
            send_gx(out1.at[n], recv1.at[n], 6 * n, half, 0)

    def middle_forward(n, scale):
        total = None
        for half in (zl, 1 - zl):
            part = recv1.at[n, pl.ds(half * 4, 4)]
            arrived(part, 6 * n + half)
            term = left3(xfh[half], xfl[half], part[...].reshape(512, 128))
            total = term if total is None else total + term
        out2[n] = total.reshape(16, 16, 128)
        over_ring(out2.at[n], recv2.at[n], 6 * n + 2)
        if n == 0:
            spread_weights()
        arrived(recv2.at[n], 6 * n + 2)
        v = left3(yfh[...], yfl[...], recv2[n].reshape(256, 128)) * scale
        return jnp.concatenate(pack_kz(v), axis=0)

    def send_back(rows, n, scale):
        planes = unpack_kz([rows[j * 32 : (j + 1) * 32] * scale for j in range(4)])
        out5[n] = left3(yih[...], yil[...], planes).reshape(16, 16, 128)
        over_ring(out5.at[n], recv5.at[n], 6 * n + 3)

    def middle_inverse(n):
        arrived(recv5.at[n], 6 * n + 3)
        high, low = split(recv5[n].reshape(256, 128))
        for half_is_own in (False, True):
            half = zl if half_is_own else 1 - zl
            for dy in (2, 1, 3, 0):
                block = half * 4 + (yp + dy) % 4
                value = dot(xih[block], high) + (dot(xil[block], high) + dot(xih[block], low))
                out6[n, block] = value.reshape(2, 8, 8, 128)
                if half_is_own and dy == 0:
                    keep_gx(out6.at[n], recv6.at[n], 6 * n + 4)
                else:
                    send_gx(out6.at[n], recv6.at[n], 6 * n + 4, half, dy)

    def depth_inverse(n, half, finish):
        arrived(recv6.at[n, pl.ds(half * 4, 4)], 6 * n + 4 + half)
        parts = []
        for r in range(2):
            parts.append(swap_groups([recv6[n, half * 4 + k, r].reshape(64, 128) for k in range(4)]))
        rows = jnp.concatenate(
            [jnp.concatenate([parts[0][cg], parts[1][cg]], axis=1) for cg in range(4)], axis=0
        )
        high, low = split(rows)
        for pair in range(4):
            cols = pl.ds(pair * 256, 256)
            value = dot(high, zih[:, cols]) + (dot(low, zih[:, cols]) + dot(high, zil[:, cols]))
            for cg in range(4):
                for k in range(2):
                    finish(
                        cg * 8 + pair * 2 + k,
                        half,
                        value[cg * 64 : (cg + 1) * 64, k * 128 : (k + 1) * 128].reshape(8, 8, 128),
                    )

    def kron(transposed):
        same = lax.broadcasted_iota(jnp.int32, (256, 256), 0) % 8 == (
            lax.broadcasted_iota(jnp.int32, (256, 256), 1) % 8
        )
        dims = (((1,), (1 if transposed else 0,)), ((), ()))
        for k, half in enumerate(split(point_ref[...])):
            tall = lax.dot_general(rows8[...], half, dims, preferred_element_type=F32).astype(BF16)
            wide = lax.dot_general(
                tall, rows8[...], (((1,), (1,)), ((), ())), preferred_element_type=F32
            )
            point_kron[k] = jnp.where(same, wide, 0.0).astype(BF16)

    def pointwise(src, dst):
        def one(x, carry):
            block = jnp.concatenate([src[:, x, yh].reshape(256, 128) for yh in range(2)], axis=1)
            value = left3(point_kron[0], point_kron[1], block)
            for yh in range(2):
                dst[:, x, yh] = value[:, yh * 128 : (yh + 1) * 128].reshape(32, 8, 128)
            return carry

        lax.fori_loop(0, 8, one, 0)

    def weight_cols(k):
        return pl.ds(pl.multiple_of(k * 2048, 2048), 2048)

    def move_weights():
        inputs[1].wait()

        def one(k):
            push(weight.at[:, weight_cols(k)], wloc.at[s, h % 4], 12, 12, mover(k))

        for k in range(1, 4):
            one((yp + k) % 4)
        pl.when(on_self)(lambda: keep(weight.at[:, weight_cols(yp)], wloc.at[s, h % 4], 12))
        pl.when(jnp.logical_not(on_self))(lambda: one(yp))

    def spread_weights():
        arrived(wloc.at[s], 12)
        for k in (2, 1, 3):
            push(wloc.at[s], wloc.at[s], 13, 13, ((s + k) % 4, gx, h))

    def wait_weights():
        arrived(wloc.at[pl.ds(0, 3)], 13)

    fetch(0).wait()
    fetch(1).wait()
    inputs[0].wait()
    depth_forward(field, 1 - zl, out1.at[0])
    pl.when(on_self)(lambda: pl.semaphore_wait(barrier, 31))
    pl.when(jnp.logical_not(on_self))(lambda: pl.semaphore_wait(barrier, 33))
    send_half(0, False)
    depth_forward(field, zl, out1.at[0])
    send_half(0, True)
    move_weights()
    for k in range(2, n_tab):
        fetch(k).wait()
    kron(False)
    pointwise(field, local)

    operands = right2(middle_forward(0, scale_cells), use[...])
    for b in range(2):
        use_ref[b] = operands[:, b * 128 : (b + 1) * 128].reshape(4, 32, 128)
    wait_weights()

    def mix(pair, total):
        cols = pl.ds(pl.multiple_of(pair * 128, 128), 128)
        tiles = [wloc[j, :, :, cols].reshape(32, 128) for j in range(4)]
        both = [
            jnp.concatenate([use_ref[b, j] * tiles[j] for j in range(4)], axis=0) for b in range(2)
        ]
        rows = pl.ds(pl.multiple_of(pair * 256, 256), 256)
        return total + right2(jnp.concatenate(both, axis=1), gather[rows])

    mixed = lax.fori_loop(0, 16, mix, jnp.zeros((128, 128), F32))
    send_back(mixed, 0, scale_modes)
    middle_inverse(0)

    inputs[2].wait()

    def slope_of(c, half, value):
        pre = value + local[c, :, half] + bias_ref[c]
        slope[c, :, half] = cot[c, :, half] * gelu_slope(pre)

    for half_is_own in (True, False):
        half = zl if half_is_own else 1 - zl
        depth_inverse(0, half, slope_of)
        depth_forward(slope, half, out1.at[1])
        send_half(1, half_is_own)
    kron(True)
    pointwise(slope, local)

    spec_high, spec_low = split(middle_forward(1, scale_modes))

    def adjoint(pair, carry):
        first, second = carry
        cols = pl.ds(pl.multiple_of(pair * 256, 256), 256)
        wide = dot(spec_high, spread[:, cols]) + dot(spec_low, spread[:, cols])
        cols = pl.ds(pl.multiple_of(pair * 128, 128), 128)
        ones, twos = [], []
        for j in range(4):
            zr = wide[j * 32 : (j + 1) * 32, :128]
            zi = wide[j * 32 : (j + 1) * 32, 128:]
            tile = wloc[j, :, :, cols].reshape(32, 128)
            ones.append(zr * tile)
            twos.append(zi * tile)
            gloc[j, :, :, cols] = (zr * use_ref[0, j] + zi * use_ref[1, j]).reshape(4, 8, 128)
        return first + jnp.concatenate(ones, axis=0), second + jnp.concatenate(twos, axis=0)

    zero = jnp.zeros((128, 128), F32)
    both = jnp.concatenate(lax.fori_loop(0, 16, adjoint, (zero, zero)), axis=1)
    send_back(right2(both, fold[...]), 1, scale_cells)
    for k in (2, 1, 3):
        to = (s + k) % 4
        push(gloc.at[to], grecv.at[k - 1], 14, 14, (to, gx, h))
    middle_inverse(1)

    arrived(grecv, 14)
    for k in range(4):
        gsum[k] = (gloc[s, k] + grecv[0, k]) + (grecv[1, k] + grecv[2, k])

    def return_sum(k):
        push(gsum.at[k], gspec.at[:, weight_cols(yp)], 15, 15, owner(k))

    for k in range(1, 4):
        return_sum((h + k) % 4)
    pl.when(on_self)(lambda: keep(gsum.at[h % 4], gspec.at[:, weight_cols(yp)], 15))
    pl.when(jnp.logical_not(on_self))(lambda: return_sum(h % 4))

    def finish(c, half, value):
        grad[c, :, half] = value + local[c, :, half]

    depth_inverse(1, zl, finish)
    depth_inverse(1, 1 - zl, finish)
    grad_out = pltpu.make_async_copy(grad, gi_hbm, done_sem.at[0])
    grad_out.start()
    arrived(gspec, 15)
    spec_out = pltpu.make_async_copy(gspec, gs_hbm, done_sem.at[1])
    spec_out.start()

    for n in range(2):
        sent(out1.at[n, pl.ds(0, 7)], 6 * n)
        sent(out2.at[n, pl.ds(0, 15)], 6 * n + 2)
        sent(out5.at[n, pl.ds(0, 15)], 6 * n + 3)
        sent(out6.at[n, pl.ds(0, 7)], 6 * n + 4)
    sent(wloc.at[pl.ds(0, 3)], 13)
    sent(gloc.at[pl.ds(0, 3)], 14)
    sent(weight.at[:, pl.ds(0, 6144)], 12)
    sent(gsum.at[pl.ds(0, 3)], 15)

    @pl.when(jnp.logical_not(on_self))
    def _():
        sent(weight.at[:, pl.ds(0, 2048)], 12)
        sent(gsum.at[0], 15)

    grad_out.wait()
    spec_out.wait()


def body(field, cotangent, spectral_weight, pointwise_weight, bias):
    shape = (C, 8, 2, 8, NZ)
    big = (2, 8, 2, 8, 8, 128)
    ring = (2, 16, 16, 128)
    rows = (4, 4, 8, 2048)
    any_spec = pl.BlockSpec(memory_space=pl.ANY)
    grad_input, grad_spectral = pl.pallas_call(
        kernel,
        out_shape=(
            jax.ShapeDtypeStruct(shape, F32),
            jax.ShapeDtypeStruct(spectral_weight.shape, F32),
        ),
        in_specs=[any_spec] * 3
        + [pl.BlockSpec(memory_space=pltpu.VMEM), pl.BlockSpec(memory_space=pltpu.SMEM)]
        + [any_spec] * len(TABLES),
        out_specs=(any_spec, any_spec),
        scratch_shapes=[pltpu.VMEM(t.shape, BF16) for t in TABLES]
        + [
            pltpu.VMEM(shape, F32),
            pltpu.VMEM(shape, F32),
            pltpu.VMEM((8, 8192), F32),
            pltpu.VMEM(shape, F32),
            pltpu.VMEM(shape, F32),
            pltpu.VMEM(shape, F32),
            pltpu.VMEM((8, 8192), F32),
            pltpu.VMEM(rows, F32),
            pltpu.VMEM(rows, F32),
            pltpu.VMEM((3,) + rows[1:], F32),
            pltpu.VMEM(rows[1:], F32),
            pltpu.VMEM((2, 256, 256), BF16),
            pltpu.VMEM((2, 4, 32, 128), F32),
            pltpu.VMEM(big, F32),
            pltpu.VMEM(big, F32),
            pltpu.VMEM(ring, F32),
            pltpu.VMEM(ring, F32),
            pltpu.VMEM(ring, F32),
            pltpu.VMEM(ring, F32),
            pltpu.VMEM(big, F32),
            pltpu.VMEM(big, F32),
            pltpu.SemaphoreType.DMA((3,)),
            pltpu.SemaphoreType.DMA((len(TABLES),)),
            pltpu.SemaphoreType.DMA((2,)),
            pltpu.SemaphoreType.DMA((16,)),
            pltpu.SemaphoreType.DMA((16,)),
        ],
        compiler_params=pltpu.CompilerParams(
            has_side_effects=True, collective_id=0, vmem_limit_bytes=63 * 1024 * 1024
        ),
        name="fno_backward",
    )(
        field.reshape(shape),
        cotangent.reshape(shape),
        spectral_weight,
        pointwise_weight,
        bias,
        *[jnp.asarray(t) for t in TABLES],
    )
    return grad_input.reshape(field.shape), grad_spectral


def solution(mesh):
    placed = (
        P("dp", None, "gx", "gy", None),
        P("dp", None, "gx", "gy", None),
        P(("gx", "gy"), "dp"),
        P(),
        P(),
    )
    return jax.shard_map(
        body,
        mesh=mesh,
        in_specs=placed,
        out_specs=(P("dp", None, "gx", "gy", None), P(("gx", "gy"), "dp")),
        check_vma=False,
    )
```

```python
import math

import jax
import jax.numpy as jnp
import numpy as np
from jax import lax
from jax.experimental import pallas as pl
from jax.experimental.pallas import tpu as pltpu
from jax.sharding import PartitionSpec as P

C = 32
MX = 16
MY = 32
MZ = 16
NX = 64
NY = 128
NZ = 128

F32 = jnp.float32
BF16 = jnp.bfloat16
MESH = pl.DeviceIdType.MESH

KX = np.array([4 * ((d // 2) % 4) + 2 * (d % 2) + d // 8 for d in range(16)])


def cos_sin(count, freqs):
    turns = np.mod(np.arange(count)[:, None] * freqs[None, :], count)
    theta = turns * (2.0 * math.pi / count)
    return np.cos(theta), np.sin(theta)


def halves(table):
    table = table.astype(np.float32)
    high = table.astype(jnp.bfloat16)
    low = (table - high.astype(np.float32)).astype(jnp.bfloat16)
    return [high, low]


def tables():
    eye8 = np.eye(8)
    cz, sz = cos_sin(NZ, np.arange(MZ))
    ztable = np.stack([cz, -sz], -1)
    cx, sx = cos_sin(NX, KX - MX // 2)
    cy, sy = cos_sin(NY, np.arange(MY) - MY // 2)

    def forward(c, s):
        return np.stack([np.stack([c, -s], -1), np.stack([s, c], -1)], -2)

    def inverse(c, s):
        return np.stack([np.stack([c, s], -1), np.stack([-s, c], -1)], -2)

    z_fwd = np.einsum("zkr,cd->czrkd", ztable, eye8).reshape(8 * NZ, 2 * MZ * 8)
    z_inv = np.ascontiguousarray(z_fwd.T)
    fx = forward(cx, sx).reshape(8, 8, 16, 2, 2)
    fx = fx.reshape(4, 2, 8, 16, 2, 2)
    x_fwd = np.einsum("gzxdrq,yw->zdqygrxw", fx, eye8).reshape(2, 256, 512)
    ix = inverse(cx, sx).reshape(8, 8, 16, 2, 2)
    ix = ix.reshape(4, 2, 8, 16, 2, 2)
    x_inv = np.einsum("gzxdqr,yw->zgrxydqw", ix, eye8).reshape(8, 128, 256)
    fy = forward(cy, sy).reshape(16, 8, MY, 2, 2)
    y_fwd = np.einsum("dyjqp->pjdqy", fy).reshape(64, 256)
    iy = inverse(cy, sy).reshape(16, 8, MY, 2, 2)
    y_inv = np.einsum("dyjpr->drypj", iy).reshape(256, 64)

    use = np.zeros((128, 2, 2, C, 2), np.float32)
    for i in range(C):
        use[i, 0, :, i, 0] = 1.0
        use[C + i, 0, :, i, 1] = -1.0
        use[C + i, 1, :, i, 0] = 1.0
        use[i, 1, :, i, 1] = 1.0
    spread = np.zeros((128, 16, 2, 2, C, 2), np.float32)
    for b in range(2):
        for o in range(C):
            spread[b * C + o, o // 2, b, o % 2] = 1.0
    spread = spread.reshape(128, 4096)
    fold = np.zeros((2, 2, C, 2, 128), np.float32)
    for i in range(C):
        fold[0, :, i, 0, i] = 1.0
        fold[1, :, i, 1, i] = 1.0
        fold[1, :, i, 0, C + i] = 1.0
        fold[0, :, i, 1, C + i] = -1.0
    rows8 = np.repeat(np.eye(C), 8, axis=0)
    out = []
    for t in (z_fwd, x_fwd, y_fwd, y_inv, x_inv, z_inv):
        out += halves(t)
    out += [
        t.astype(jnp.bfloat16)
        for t in (
            use.reshape(128, 256),
            spread,
            np.ascontiguousarray(spread.T),
            fold.reshape(256, 128),
            rows8,
        )
    ]
    return out


TABLES = tables()


def gelu_slope(values):
    normal_cdf = 0.5 * (1.0 + lax.erf(values * math.sqrt(0.5)))
    return normal_cdf + values * jnp.exp(-0.5 * values * values) * (1.0 / math.sqrt(2.0 * math.pi))


def split(x):
    high = x.astype(BF16)
    return high, (x - high.astype(F32)).astype(BF16)


def dot(a, b):
    return jnp.dot(a, b, preferred_element_type=F32)


def left3(high, low, x):
    xh, xl = split(x)
    return dot(high, xh) + (dot(low, xh) + dot(high, xl))


def right3(x, high, low):
    xh, xl = split(x)
    return dot(xh, high) + (dot(xl, high) + dot(xh, low))


def right2(x, table):
    xh, xl = split(x)
    return dot(xh, table) + dot(xl, table)


def lanes_of(rows):
    return lax.broadcasted_iota(jnp.int32, (rows, 128), 1)


def roll(x, shift):
    shift = shift % 128
    return pltpu.roll(x, shift, axis=1) if shift else x


def swap_groups(blocks):
    group = (lanes_of(64) % 32) // 8
    out = []
    for a in range(4):
        total = blocks[a]
        for b in range(4):
            if b != a:
                total = jnp.where(group == b, roll(blocks[b], (b - a) * 8), total)
        out.append(total)
    return out


def pack_kz(v):
    lane = lanes_of(32)
    return [
        jnp.where(lane < 32, roll(v[:32], -j * 32), roll(v[32:], 32 - j * 32)) for j in range(4)
    ]


def unpack_kz(blocks):
    lane = lanes_of(32)
    parts = []
    for p in range(2):
        total = jnp.zeros((32, 128), F32)
        for j in range(4):
            total = total + jnp.where(lane // 32 == j, roll(blocks[j], (j - p) * 32), 0.0)
        parts.append(total)
    return jnp.concatenate(parts, axis=0)


def kernel(
    field_hbm,
    cot_hbm,
    weight_hbm,
    point_ref,
    bias_ref,
    *rest,
):
    n_tab = len(TABLES)
    tab_hbm = rest[:n_tab]
    gi_hbm, gs_hbm = rest[n_tab : n_tab + 2]
    scratch = rest[n_tab + 2 :]
    tab = scratch[:n_tab]
    (
        field,
        cot,
        weight,
        local,
        slope,
        grad,
        gspec,
        wloc,
        gloc,
        grecv,
        gsum,
        point_kron,
        use_ref,
        out1,
        recv1,
        out2,
        recv2,
        out5,
        recv5,
        out6,
        recv6,
        in_sem,
        tab_sem,
        done_sem,
        send_sem,
        recv_sem,
    ) = scratch[n_tab:]
    (zfh, zfl, xfh, xfl, yfh, yfl, yih, yil, xih, xil, zih, zil, use, spread, gather, fold, rows8) = tab

    s = lax.axis_index("dp")
    gx = lax.axis_index("gx")
    h = lax.axis_index("gy")
    yp = gx // 2
    zl = gx % 2
    place = 2 * h + zl
    on_self = yp == h % 4
    scale_cells = 1.0 / math.sqrt(NX * NY * NZ)
    scale_modes = 1.0 / math.sqrt(MX * MY * MZ)

    def mover(k):
        return (s, 2 * k + zl, (h // 4) * 4 + yp)

    def owner(k):
        return (s, 2 * (h % 4) + zl, (h // 4) * 4 + k)

    barrier = pltpu.get_barrier_semaphore()

    def hello(device):
        pl.semaphore_signal(barrier, inc=1, device_id=device, device_id_type=MESH)

    for k in range(1, 16):
        to = (place + k) % 16
        hello((s, 2 * yp + to % 2, to // 2))
    for k in range(1, 8):
        hello((s, (gx + k) % 8, h))
    for k in range(1, 4):
        hello(((s + k) % 4, gx, h))
        hello(mover((yp + k) % 4))
        hello(owner((h + k) % 4))

    @pl.when(jnp.logical_not(on_self))
    def _():
        hello(mover(yp))
        hello(owner(h % 4))

    def fetch(k):
        return pltpu.make_async_copy(tab_hbm[k], tab[k], tab_sem.at[k])

    inputs = [
        pltpu.make_async_copy(a, b, in_sem.at[k])
        for k, (a, b) in enumerate(((field_hbm, field), (weight_hbm, weight), (cot_hbm, cot)))
    ]
    fetch(0).start()
    fetch(1).start()
    inputs[0].start()
    inputs[1].start()
    for k in range(2, n_tab):
        fetch(k).start()
    inputs[2].start()

    def push(src, dst, out_sem, in_sem, device):
        pltpu.make_async_remote_copy(
            src_ref=src,
            dst_ref=dst,
            send_sem=send_sem.at[out_sem],
            recv_sem=recv_sem.at[in_sem],
            device_id=device,
            device_id_type=MESH,
        ).start()

    def keep(src, dst, in_sem):
        pltpu.make_async_copy(src, dst, recv_sem.at[in_sem]).start()

    def arrived(buffer, in_sem):
        pltpu.make_async_copy(buffer, buffer, recv_sem.at[in_sem]).wait()

    def sent(buffer, out_sem):
        pltpu.make_async_copy(buffer, buffer, send_sem.at[out_sem]).wait()

    def send_gx(src, dst, stage, to_zl, dy):
        to_yp = (yp + dy) % 4
        block = to_zl * 4 + to_yp
        push(src.at[block], dst.at[zl * 4 + yp], stage, stage + zl, (s, 2 * to_yp + to_zl, h))

    def keep_gx(src, dst, stage):
        block = zl * 4 + yp
        keep(src.at[block], dst.at[block], stage + zl)

    def over_ring(src, dst, stage):
        for k in (8, 7, 9, 6, 10, 5, 11, 4, 12, 3, 13, 2, 14, 1, 15):
            to = (place + k) % 16
            push(src.at[to], dst.at[place], stage, stage, (s, 2 * yp + to % 2, to // 2))
        keep(src.at[place], dst.at[place], stage)

    def depth_forward(grid, half, dst):
        total = jnp.zeros((256, 256), F32)
        for pair in range(4):
            block = jnp.concatenate(
                [
                    jnp.concatenate(
                        [grid[cg * 8 + pair * 2 + k, :, half].reshape(64, 128) for k in range(2)], axis=1
                    )
                    for cg in range(4)
                ],
                axis=0,
            )
            rows = pl.ds(pair * 256, 256)
            total = total + right3(block, zfh[rows], zfl[rows])
        for r in range(2):
            blocks = [total[cg * 64 : (cg + 1) * 64, r * 128 : (r + 1) * 128] for cg in range(4)]
            for k, block in enumerate(swap_groups(blocks)):
                dst[half * 4 + k, r] = block.reshape(8, 8, 128)

    def send_half(n, half_is_own):
        half = zl if half_is_own else 1 - zl
        for dy in (2, 1, 3):
            send_gx(out1.at[n], recv1.at[n], 6 * n, half, dy)
        if half_is_own:
            keep_gx(out1.at[n], recv1.at[n], 6 * n)
        else:
            send_gx(out1.at[n], recv1.at[n], 6 * n, half, 0)

    def middle_forward(n, scale):
        total = None
        for half in (zl, 1 - zl):
            part = recv1.at[n, pl.ds(half * 4, 4)]
            arrived(part, 6 * n + half)
            term = left3(xfh[half], xfl[half], part[...].reshape(512, 128))
            total = term if total is None else total + term
        out2[n] = total.reshape(16, 16, 128)
        over_ring(out2.at[n], recv2.at[n], 6 * n + 2)
        arrived(recv2.at[n], 6 * n + 2)
        v = left3(yfh[...], yfl[...], recv2[n].reshape(256, 128)) * scale
        return jnp.concatenate(pack_kz(v), axis=0)

    def send_back(rows, n, scale):
        planes = unpack_kz([rows[j * 32 : (j + 1) * 32] * scale for j in range(4)])
        out5[n] = left3(yih[...], yil[...], planes).reshape(16, 16, 128)
        over_ring(out5.at[n], recv5.at[n], 6 * n + 3)

    def middle_inverse(n):
        arrived(recv5.at[n], 6 * n + 3)
        high, low = split(recv5[n].reshape(256, 128))
        for half_is_own in (False, True):
            half = zl if half_is_own else 1 - zl
            for dy in (2, 1, 3, 0):
                block = half * 4 + (yp + dy) % 4
                value = dot(xih[block], high) + (dot(xil[block], high) + dot(xih[block], low))
                out6[n, block] = value.reshape(2, 8, 8, 128)
                if half_is_own and dy == 0:
                    keep_gx(out6.at[n], recv6.at[n], 6 * n + 4)
                else:
                    send_gx(out6.at[n], recv6.at[n], 6 * n + 4, half, dy)

    def depth_inverse(n, half, finish):
        arrived(recv6.at[n, pl.ds(half * 4, 4)], 6 * n + 4 + half)
        parts = []
        for r in range(2):
            parts.append(swap_groups([recv6[n, half * 4 + k, r].reshape(64, 128) for k in range(4)]))
        rows = jnp.concatenate(
            [jnp.concatenate([parts[0][cg], parts[1][cg]], axis=1) for cg in range(4)], axis=0
        )
        high, low = split(rows)
        for pair in range(4):
            cols = pl.ds(pair * 256, 256)
            value = dot(high, zih[:, cols]) + (dot(low, zih[:, cols]) + dot(high, zil[:, cols]))
            for cg in range(4):
                for k in range(2):
                    finish(
                        cg * 8 + pair * 2 + k,
                        half,
                        value[cg * 64 : (cg + 1) * 64, k * 128 : (k + 1) * 128].reshape(8, 8, 128),
                    )

    def kron(transposed):
        same = lax.broadcasted_iota(jnp.int32, (256, 256), 0) % 8 == (
            lax.broadcasted_iota(jnp.int32, (256, 256), 1) % 8
        )
        dims = (((1,), (1 if transposed else 0,)), ((), ()))
        for k, half in enumerate(split(point_ref[...])):
            tall = lax.dot_general(rows8[...], half, dims, preferred_element_type=F32).astype(BF16)
            wide = lax.dot_general(
                tall, rows8[...], (((1,), (1,)), ((), ())), preferred_element_type=F32
            )
            point_kron[k] = jnp.where(same, wide, 0.0).astype(BF16)

    def pointwise(src, dst):
        def one(x, carry):
            block = jnp.concatenate([src[:, x, yh].reshape(256, 128) for yh in range(2)], axis=1)
            value = left3(point_kron[0], point_kron[1], block)
            for yh in range(2):
                dst[:, x, yh] = value[:, yh * 128 : (yh + 1) * 128].reshape(32, 8, 128)
            return carry

        lax.fori_loop(0, 8, one, 0)

    def weight_cols(k):
        return pl.ds(pl.multiple_of(k * 2048, 2048), 2048)

    def move_weights():
        inputs[1].wait()

        def one(k):
            push(weight.at[:, weight_cols(k)], wloc.at[s, h % 4], 12, 12, mover(k))

        for k in range(1, 4):
            one((yp + k) % 4)
        pl.when(on_self)(lambda: keep(weight.at[:, weight_cols(yp)], wloc.at[s, h % 4], 12))
        pl.when(jnp.logical_not(on_self))(lambda: one(yp))

    def spread_weights():
        arrived(wloc.at[s], 12)
        for k in (2, 1, 3):
            push(wloc.at[s], wloc.at[s], 13, 13, ((s + k) % 4, gx, h))

    def wait_weights():
        arrived(wloc.at[pl.ds(0, 3)], 13)

    fetch(0).wait()
    fetch(1).wait()
    inputs[0].wait()
    depth_forward(field, 1 - zl, out1.at[0])
    pl.when(on_self)(lambda: pl.semaphore_wait(barrier, 31))
    pl.when(jnp.logical_not(on_self))(lambda: pl.semaphore_wait(barrier, 33))
    move_weights()
    send_half(0, False)
    depth_forward(field, zl, out1.at[0])
    send_half(0, True)
    for k in range(2, n_tab):
        fetch(k).wait()
    kron(False)
    spread_weights()
    pointwise(field, local)

    operands = right2(middle_forward(0, scale_cells), use[...])
    for b in range(2):
        use_ref[b] = operands[:, b * 128 : (b + 1) * 128].reshape(4, 32, 128)
    wait_weights()

    def mix(pair, total):
        cols = pl.ds(pair * 128, 128)
        tiles = [wloc[j, :, :, cols].reshape(32, 128) for j in range(4)]
        both = [
            jnp.concatenate([use_ref[b, j] * tiles[j] for j in range(4)], axis=0) for b in range(2)
        ]
        rows = pl.ds(pair * 256, 256)
        return total + right2(jnp.concatenate(both, axis=1), gather[rows])

    mixed = jnp.zeros((128, 128), F32)
    for pair in range(16):
        mixed = mix(pair, mixed)
    send_back(mixed, 0, scale_modes)
    middle_inverse(0)

    inputs[2].wait()

    def slope_of(c, half, value):
        pre = value + local[c, :, half] + bias_ref[c]
        slope[c, :, half] = cot[c, :, half] * gelu_slope(pre)

    for half_is_own in (True, False):
        half = zl if half_is_own else 1 - zl
        depth_inverse(0, half, slope_of)
        depth_forward(slope, half, out1.at[1])
        send_half(1, half_is_own)
    kron(True)
    pointwise(slope, local)

    spec_high, spec_low = split(middle_forward(1, scale_modes))

    def adjoint(pair, carry):
        first, second = carry
        cols = pl.ds(pair * 256, 256)
        wide = dot(spec_high, spread[:, cols]) + dot(spec_low, spread[:, cols])
        cols = pl.ds(pair * 128, 128)
        ones, twos = [], []
        for j in range(4):
            zr = wide[j * 32 : (j + 1) * 32, :128]
            zi = wide[j * 32 : (j + 1) * 32, 128:]
            tile = wloc[j, :, :, cols].reshape(32, 128)
            ones.append(zr * tile)
            twos.append(zi * tile)
            gloc[j, :, :, cols] = (zr * use_ref[0, j] + zi * use_ref[1, j]).reshape(4, 8, 128)
        return first + jnp.concatenate(ones, axis=0), second + jnp.concatenate(twos, axis=0)

    sums = (jnp.zeros((128, 128), F32),) * 2
    for pair in range(16):
        sums = adjoint(pair, sums)
    both = jnp.concatenate(sums, axis=1)
    send_back(right2(both, fold[...]), 1, scale_cells)
    for part in range(4):
        for k in (2, 1, 3):
            to = (s + k) % 4
            push(gloc.at[to, part], grecv.at[part, k - 1], 14, 16 + part, (to, gx, h))
    middle_inverse(1)

    for part in range(4):
        arrived(grecv.at[part], 16 + part)
        gsum[part] = (gloc[s, part] + grecv[part, 0]) + (grecv[part, 1] + grecv[part, 2])
        own = jnp.logical_and(on_self, h % 4 == part)
        target = gspec.at[:, weight_cols(yp)]
        pl.when(own)(lambda: keep(gsum.at[part], target, 15))
        pl.when(jnp.logical_not(own))(lambda: push(gsum.at[part], target, 15, 15, owner(part)))

    def finish(c, half, value):
        grad[c, :, half] = value + local[c, :, half]

    depth_inverse(1, zl, finish)
    depth_inverse(1, 1 - zl, finish)
    grad_out = pltpu.make_async_copy(grad, gi_hbm, done_sem.at[0])
    grad_out.start()
    arrived(gspec, 15)
    spec_out = pltpu.make_async_copy(gspec, gs_hbm, done_sem.at[1])
    spec_out.start()

    for n in range(2):
        sent(out1.at[n, pl.ds(0, 7)], 6 * n)
        sent(out2.at[n, pl.ds(0, 15)], 6 * n + 2)
        sent(out5.at[n, pl.ds(0, 15)], 6 * n + 3)
        sent(out6.at[n, pl.ds(0, 7)], 6 * n + 4)
    sent(wloc.at[pl.ds(0, 3)], 13)
    sent(gloc.at[pl.ds(0, 3)], 14)
    sent(weight.at[:, pl.ds(0, 6144)], 12)
    sent(gsum.at[pl.ds(0, 3)], 15)

    @pl.when(jnp.logical_not(on_self))
    def _():
        sent(weight.at[:, pl.ds(0, 2048)], 12)
        sent(gsum.at[0], 15)

    grad_out.wait()
    spec_out.wait()


def body(field, cotangent, spectral_weight, pointwise_weight, bias):
    shape = (C, 8, 2, 8, NZ)
    big = (2, 8, 2, 8, 8, 128)
    ring = (2, 16, 16, 128)
    rows = (4, 4, 8, 2048)
    any_spec = pl.BlockSpec(memory_space=pl.ANY)
    grad_input, grad_spectral = pl.pallas_call(
        kernel,
        out_shape=(
            jax.ShapeDtypeStruct(shape, F32),
            jax.ShapeDtypeStruct(spectral_weight.shape, F32),
        ),
        in_specs=[any_spec] * 3
        + [pl.BlockSpec(memory_space=pltpu.VMEM), pl.BlockSpec(memory_space=pltpu.SMEM)]
        + [any_spec] * len(TABLES),
        out_specs=(any_spec, any_spec),
        scratch_shapes=[pltpu.VMEM(t.shape, BF16) for t in TABLES]
        + [
            pltpu.VMEM(shape, F32),
            pltpu.VMEM(shape, F32),
            pltpu.VMEM((8, 8192), F32),
            pltpu.VMEM(shape, F32),
            pltpu.VMEM(shape, F32),
            pltpu.VMEM(shape, F32),
            pltpu.VMEM((8, 8192), F32),
            pltpu.VMEM(rows, F32),
            pltpu.VMEM(rows, F32),
            pltpu.VMEM((4, 3, 8, 2048), F32),
            pltpu.VMEM(rows[1:], F32),
            pltpu.VMEM((2, 256, 256), BF16),
            pltpu.VMEM((2, 4, 32, 128), F32),
            pltpu.VMEM(big, F32),
            pltpu.VMEM(big, F32),
            pltpu.VMEM(ring, F32),
            pltpu.VMEM(ring, F32),
            pltpu.VMEM(ring, F32),
            pltpu.VMEM(ring, F32),
            pltpu.VMEM(big, F32),
            pltpu.VMEM(big, F32),
            pltpu.SemaphoreType.DMA((3,)),
            pltpu.SemaphoreType.DMA((len(TABLES),)),
            pltpu.SemaphoreType.DMA((2,)),
            pltpu.SemaphoreType.DMA((16,)),
            pltpu.SemaphoreType.DMA((20,)),
        ],
        compiler_params=pltpu.CompilerParams(
            has_side_effects=True, collective_id=0, vmem_limit_bytes=63 * 1024 * 1024
        ),
        name="fno_backward",
    )(
        field.reshape(shape),
        cotangent.reshape(shape),
        spectral_weight,
        pointwise_weight,
        bias,
        *[jnp.asarray(t) for t in TABLES],
    )
    return grad_input.reshape(field.shape), grad_spectral


def solution(mesh):
    placed = (
        P("dp", None, "gx", "gy", None),
        P("dp", None, "gx", "gy", None),
        P(("gx", "gy"), "dp"),
        P(),
        P(),
    )
    return jax.shard_map(
        body,
        mesh=mesh,
        in_specs=placed,
        out_specs=(P("dp", None, "gx", "gy", None), P(("gx", "gy"), "dp")),
        check_vma=False,
    )
```

```python
import math

import jax
import jax.numpy as jnp
import numpy as np
from jax import lax
from jax.experimental import pallas as pl
from jax.experimental.pallas import tpu as pltpu
from jax.sharding import PartitionSpec as P

C = 32
MX = 16
MY = 32
MZ = 16
NX = 64
NY = 128
NZ = 128

F32 = jnp.float32
BF16 = jnp.bfloat16
MESH = pl.DeviceIdType.MESH

KX = np.array([4 * ((d // 2) % 4) + 2 * (d % 2) + d // 8 for d in range(16)])

FAR_FIRST = (8, 7, 9, 6, 10, 5, 11, 4, 12, 3, 13, 2, 14, 1, 15)


def cos_sin(count, freqs):
    turns = np.mod(np.arange(count)[:, None] * freqs[None, :], count)
    theta = turns * (2.0 * math.pi / count)
    return np.cos(theta), np.sin(theta)


def halves(table):
    table = table.astype(np.float32)
    high = table.astype(jnp.bfloat16)
    low = (table - high.astype(np.float32)).astype(jnp.bfloat16)
    return [high, low]


def tables():
    eye8 = np.eye(8)
    cz, sz = cos_sin(NZ, np.arange(MZ))
    ztable = np.stack([cz, -sz], -1)
    cx, sx = cos_sin(NX, KX - MX // 2)
    cy, sy = cos_sin(NY, np.arange(MY) - MY // 2)

    def forward(c, s):
        return np.stack([np.stack([c, -s], -1), np.stack([s, c], -1)], -2)

    def inverse(c, s):
        return np.stack([np.stack([c, s], -1), np.stack([-s, c], -1)], -2)

    z_fwd = np.einsum("zkr,cd->czrkd", ztable, eye8).reshape(8 * NZ, 2 * MZ * 8)
    z_inv = np.ascontiguousarray(z_fwd.T)
    fx = forward(cx, sx).reshape(8, 8, 16, 2, 2)
    fx = fx.reshape(4, 2, 8, 16, 2, 2)
    x_fwd = np.einsum("gzxdrq,yw->zdqygrxw", fx, eye8).reshape(2, 256, 512)
    ix = inverse(cx, sx).reshape(8, 8, 16, 2, 2)
    ix = ix.reshape(4, 2, 8, 16, 2, 2)
    x_inv = np.einsum("gzxdqr,yw->zgrxydqw", ix, eye8).reshape(8, 128, 256)
    fy = forward(cy, sy).reshape(16, 8, MY, 2, 2)
    y_fwd = np.einsum("dyjqp->pjdqy", fy).reshape(64, 256)
    iy = inverse(cy, sy).reshape(16, 8, MY, 2, 2)
    y_inv = np.einsum("dyjpr->drypj", iy).reshape(256, 64)

    use = np.zeros((128, 2, 2, C, 2), np.float32)
    for i in range(C):
        use[i, 0, :, i, 0] = 1.0
        use[C + i, 0, :, i, 1] = -1.0
        use[C + i, 1, :, i, 0] = 1.0
        use[i, 1, :, i, 1] = 1.0
    spread = np.zeros((128, 16, 2, 2, C, 2), np.float32)
    for b in range(2):
        for o in range(C):
            spread[b * C + o, o // 2, b, o % 2] = 1.0
    spread = spread.reshape(128, 4096)
    fold = np.zeros((2, 2, C, 2, 128), np.float32)
    for i in range(C):
        fold[0, :, i, 0, i] = 1.0
        fold[1, :, i, 1, i] = 1.0
        fold[1, :, i, 0, C + i] = 1.0
        fold[0, :, i, 1, C + i] = -1.0
    rows8 = np.repeat(np.eye(C), 8, axis=0)
    out = []
    for t in (z_fwd, z_inv):
        out += halves(t)
    for t in (x_fwd, y_fwd, y_inv, x_inv):
        out.append(np.concatenate(halves(t), axis=-2))
    out += [
        t.astype(jnp.bfloat16)
        for t in (
            use.reshape(128, 256),
            spread,
            np.ascontiguousarray(spread.T),
            fold.reshape(256, 128),
            rows8,
        )
    ]
    return out


TABLES = tables()


def gelu_slope(values):
    normal_cdf = 0.5 * (1.0 + lax.erf(values * math.sqrt(0.5)))
    return normal_cdf + values * jnp.exp(-0.5 * values * values) * (1.0 / math.sqrt(2.0 * math.pi))


def split(x):
    high = x.astype(BF16)
    return high, (x - high.astype(F32)).astype(BF16)


def dot(a, b):
    return jnp.dot(a, b, preferred_element_type=F32)


def left3(table, x):
    half = table.shape[0] // 2
    y = dot(table, jnp.concatenate(split(x), axis=1))
    return y[:half, :128] + (y[half:, :128] + y[:half, 128:])


def right2(x, table):
    half = x.shape[0]
    y = dot(jnp.concatenate(split(x), axis=0), table)
    return y[:half] + y[half:]


def right3(x, high, low):
    half = x.shape[0]
    xh, xl = split(x)
    y = dot(jnp.concatenate([xh, xl], axis=0), high)
    return y[:half] + (y[half:] + dot(xh, low))


def lanes_of(rows):
    return lax.broadcasted_iota(jnp.int32, (rows, 128), 1)


def roll(x, shift):
    shift = shift % 128
    return pltpu.roll(x, shift, axis=1) if shift else x


def swap_groups(blocks):
    group = (lanes_of(64) % 32) // 8
    out = []
    for a in range(4):
        total = blocks[a]
        for b in range(4):
            if b != a:
                total = jnp.where(group == b, roll(blocks[b], (b - a) * 8), total)
        out.append(total)
    return out


def pack_kz(v):
    lane = lanes_of(32)
    return [
        jnp.where(lane < 32, roll(v[:32], -j * 32), roll(v[32:], 32 - j * 32)) for j in range(4)
    ]


def unpack_kz(blocks):
    lane = lanes_of(32)
    parts = []
    for p in range(2):
        total = jnp.zeros((32, 128), F32)
        for j in range(4):
            total = total + jnp.where(lane // 32 == j, roll(blocks[j], (j - p) * 32), 0.0)
        parts.append(total)
    return jnp.concatenate(parts, axis=0)


def kernel(
    field_hbm,
    cot_hbm,
    weight_hbm,
    point_ref,
    bias_ref,
    *rest,
):
    n_tab = len(TABLES)
    tab_hbm = rest[:n_tab]
    gi_hbm, gs_hbm = rest[n_tab : n_tab + 2]
    scratch = rest[n_tab + 2 :]
    tab = scratch[:n_tab]
    (
        field,
        cot,
        weight,
        local,
        slope,
        grad,
        gspec,
        wloc,
        gloc,
        grecv,
        gsum,
        point_kron,
        use_ref,
        out1,
        recv1,
        out2,
        recv2,
        out5,
        recv5,
        out6,
        recv6,
        in_sem,
        tab_sem,
        done_sem,
        send_sem,
        recv_sem,
    ) = scratch[n_tab:]
    (zfh, zfl, zih, zil, xf, yf, yi, xi, use, spread, gather, fold, rows8) = tab

    s = lax.axis_index("dp")
    gx = lax.axis_index("gx")
    h = lax.axis_index("gy")
    yp = gx // 2
    zl = gx % 2
    place = 2 * h + zl
    on_self = yp == h % 4
    scale_cells = 1.0 / math.sqrt(NX * NY * NZ)
    scale_modes = 1.0 / math.sqrt(MX * MY * MZ)

    def mover(k):
        return (s, 2 * k + zl, (h // 4) * 4 + yp)

    def owner(k):
        return (s, 2 * (h % 4) + zl, (h // 4) * 4 + k)

    barrier = pltpu.get_barrier_semaphore()

    def hello(device):
        pl.semaphore_signal(barrier, inc=1, device_id=device, device_id_type=MESH)

    for k in FAR_FIRST:
        to = (place + k) % 16
        hello((s, 2 * yp + to % 2, to // 2))
    for k in range(1, 8):
        hello((s, (gx + k) % 8, h))
    for k in range(1, 4):
        hello(((s + k) % 4, gx, h))
        hello(mover((yp + k) % 4))
        hello(owner((h + k) % 4))

    @pl.when(jnp.logical_not(on_self))
    def _():
        hello(mover(yp))
        hello(owner(h % 4))

    def fetch(k):
        return pltpu.make_async_copy(tab_hbm[k], tab[k], tab_sem.at[k])

    inputs = [
        pltpu.make_async_copy(a, b, in_sem.at[k])
        for k, (a, b) in enumerate(((field_hbm, field), (weight_hbm, weight), (cot_hbm, cot)))
    ]
    fetch(0).start()
    fetch(1).start()
    inputs[0].start()
    inputs[1].start()
    for k in range(2, n_tab):
        fetch(k).start()
    inputs[2].start()

    def push(src, dst, out_sem, in_sem, device):
        pltpu.make_async_remote_copy(
            src_ref=src,
            dst_ref=dst,
            send_sem=send_sem.at[out_sem],
            recv_sem=recv_sem.at[in_sem],
            device_id=device,
            device_id_type=MESH,
        ).start()

    def keep(src, dst, in_sem):
        pltpu.make_async_copy(src, dst, recv_sem.at[in_sem]).start()

    def arrived(buffer, in_sem):
        pltpu.make_async_copy(buffer, buffer, recv_sem.at[in_sem]).wait()

    def sent(buffer, out_sem):
        pltpu.make_async_copy(buffer, buffer, send_sem.at[out_sem]).wait()

    def send_gx(src, dst, stage, to_zl, dy):
        to_yp = (yp + dy) % 4
        block = to_zl * 4 + to_yp
        push(src.at[block], dst.at[zl * 4 + yp], stage, stage + zl, (s, 2 * to_yp + to_zl, h))

    def keep_gx(src, dst, stage):
        block = zl * 4 + yp
        keep(src.at[block], dst.at[block], stage + zl)

    def over_ring(src, dst, stage):
        for k in FAR_FIRST:
            to = (place + k) % 16
            push(src.at[to], dst.at[place], stage, stage, (s, 2 * yp + to % 2, to // 2))
        keep(src.at[place], dst.at[place], stage)

    def depth_forward(grid, half, dst):
        total = jnp.zeros((256, 256), F32)
        for pair in range(4):
            block = jnp.concatenate(
                [
                    jnp.concatenate(
                        [grid[cg * 8 + pair * 2 + k, :, half].reshape(64, 128) for k in range(2)], axis=1
                    )
                    for cg in range(4)
                ],
                axis=0,
            )
            rows = pl.ds(pair * 256, 256)
            total = total + right3(block, zfh[rows], zfl[rows])
        for r in range(2):
            blocks = [total[cg * 64 : (cg + 1) * 64, r * 128 : (r + 1) * 128] for cg in range(4)]
            for k, block in enumerate(swap_groups(blocks)):
                dst[half * 4 + k, r] = block.reshape(8, 8, 128)

    def send_half(n, half_is_own):
        half = zl if half_is_own else 1 - zl
        for dy in (2, 1, 3):
            send_gx(out1.at[n], recv1.at[n], 6 * n, half, dy)
        if half_is_own:
            keep_gx(out1.at[n], recv1.at[n], 6 * n)
        else:
            send_gx(out1.at[n], recv1.at[n], 6 * n, half, 0)

    def middle_forward(n, scale):
        total = None
        for half in (zl, 1 - zl):
            part = recv1.at[n, pl.ds(half * 4, 4)]
            arrived(part, 6 * n + half)
            term = left3(xf[half], part[...].reshape(512, 128))
            total = term if total is None else total + term
        out2[n] = total.reshape(16, 16, 128)
        over_ring(out2.at[n], recv2.at[n], 6 * n + 2)
        arrived(recv2.at[n], 6 * n + 2)
        v = left3(yf[...], recv2[n].reshape(256, 128)) * scale
        return jnp.concatenate(pack_kz(v), axis=0)

    def send_back(rows, n, scale):
        planes = unpack_kz([rows[j * 32 : (j + 1) * 32] * scale for j in range(4)])
        out5[n] = left3(yi[...], planes).reshape(16, 16, 128)
        over_ring(out5.at[n], recv5.at[n], 6 * n + 3)

    def middle_inverse(n):
        arrived(recv5.at[n], 6 * n + 3)
        rows = jnp.concatenate(split(recv5[n].reshape(256, 128)), axis=1)
        for half_is_own in (False, True):
            half = zl if half_is_own else 1 - zl
            for dy in (2, 1, 3, 0):
                block = half * 4 + (yp + dy) % 4
                value = dot(xi[block], rows)
                value = value[:128, :128] + (value[128:, :128] + value[:128, 128:])
                out6[n, block] = value.reshape(2, 8, 8, 128)
                if half_is_own and dy == 0:
                    keep_gx(out6.at[n], recv6.at[n], 6 * n + 4)
                else:
                    send_gx(out6.at[n], recv6.at[n], 6 * n + 4, half, dy)

    def depth_inverse(n, half, finish):
        arrived(recv6.at[n, pl.ds(half * 4, 4)], 6 * n + 4 + half)
        parts = []
        for r in range(2):
            parts.append(swap_groups([recv6[n, half * 4 + k, r].reshape(64, 128) for k in range(4)]))
        rows = jnp.concatenate(
            [jnp.concatenate([parts[0][cg], parts[1][cg]], axis=1) for cg in range(4)], axis=0
        )
        for pair in range(4):
            cols = pl.ds(pair * 256, 256)
            value = right3(rows, zih[:, cols], zil[:, cols])
            for cg in range(4):
                for k in range(2):
                    finish(
                        cg * 8 + pair * 2 + k,
                        half,
                        value[cg * 64 : (cg + 1) * 64, k * 128 : (k + 1) * 128].reshape(8, 8, 128),
                    )

    def kron(transposed):
        same = lax.broadcasted_iota(jnp.int32, (256, 256), 0) % 8 == (
            lax.broadcasted_iota(jnp.int32, (256, 256), 1) % 8
        )
        dims = (((1,), (1 if transposed else 0,)), ((), ()))
        for k, half in enumerate(split(point_ref[...])):
            tall = lax.dot_general(rows8[...], half, dims, preferred_element_type=F32).astype(BF16)
            wide = lax.dot_general(
                tall, rows8[...], (((1,), (1,)), ((), ())), preferred_element_type=F32
            )
            point_kron[k] = jnp.where(same, wide, 0.0).astype(BF16)

    def pointwise(src, dst):
        def one(x, carry):
            block = jnp.concatenate([src[:, x, yh].reshape(256, 128) for yh in range(2)], axis=1)
            high, low = split(block)
            value = dot(point_kron[0], high) + (dot(point_kron[1], high) + dot(point_kron[0], low))
            for yh in range(2):
                dst[:, x, yh] = value[:, yh * 128 : (yh + 1) * 128].reshape(32, 8, 128)
            return carry

        lax.fori_loop(0, 8, one, 0)

    def weight_cols(k):
        return pl.ds(pl.multiple_of(k * 2048, 2048), 2048)

    def move_weights():
        inputs[1].wait()

        def one(k):
            push(weight.at[:, weight_cols(k)], wloc.at[s, h % 4], 12, 20 + h % 4, mover(k))

        for k in range(1, 4):
            one((yp + k) % 4)
        pl.when(on_self)(lambda: keep(weight.at[:, weight_cols(yp)], wloc.at[s, h % 4], 20 + h % 4))
        pl.when(jnp.logical_not(on_self))(lambda: one(yp))

    def spread_weights():
        for part in (h % 4, (h // 2 % 2) * 2 + 1 - h % 2, (1 - h // 2 % 2) * 2 + h % 2, 3 - h % 4):
            block = wloc.at[s, part]
            arrived(block, 20 + part)
            for k in (2, 1, 3):
                push(block, block, 13, 13, ((s + k) % 4, gx, h))

    def wait_weights():
        arrived(wloc.at[pl.ds(0, 3)], 13)

    fetch(0).wait()
    fetch(1).wait()
    inputs[0].wait()
    depth_forward(field, 1 - zl, out1.at[0])
    pl.when(on_self)(lambda: pl.semaphore_wait(barrier, 31))
    pl.when(jnp.logical_not(on_self))(lambda: pl.semaphore_wait(barrier, 33))
    move_weights()
    send_half(0, False)
    depth_forward(field, zl, out1.at[0])
    send_half(0, True)
    spread_weights()
    for k in range(2, n_tab):
        fetch(k).wait()
    kron(False)
    pointwise(field, local)

    operands = right2(middle_forward(0, scale_cells), use[...])
    for b in range(2):
        use_ref[b] = operands[:, b * 128 : (b + 1) * 128].reshape(4, 32, 128)
    wait_weights()

    def mix(pair, total):
        cols = pl.ds(pair * 128, 128)
        tiles = [wloc[j, :, :, cols].reshape(32, 128) for j in range(4)]
        both = [
            jnp.concatenate([use_ref[b, j] * tiles[j] for j in range(4)], axis=0) for b in range(2)
        ]
        rows = pl.ds(pair * 256, 256)
        return total + right2(jnp.concatenate(both, axis=1), gather[rows])

    mixed = jnp.zeros((128, 128), F32)
    for pair in range(16):
        mixed = mix(pair, mixed)
    send_back(mixed, 0, scale_modes)
    middle_inverse(0)

    inputs[2].wait()

    def slope_of(c, half, value):
        pre = value + local[c, :, half] + bias_ref[c]
        slope[c, :, half] = cot[c, :, half] * gelu_slope(pre)

    for half_is_own in (True, False):
        half = zl if half_is_own else 1 - zl
        depth_inverse(0, half, slope_of)
        depth_forward(slope, half, out1.at[1])
        send_half(1, half_is_own)
    kron(True)
    pointwise(slope, local)

    spectra = jnp.concatenate(split(middle_forward(1, scale_modes)), axis=0)

    def adjoint(pair, carry):
        first, second = carry
        cols = pl.ds(pair * 256, 256)
        wide = dot(spectra, spread[:, cols])
        wide = wide[:128] + wide[128:]
        cols = pl.ds(pair * 128, 128)
        ones, twos = [], []
        for j in range(4):
            zr = wide[j * 32 : (j + 1) * 32, :128]
            zi = wide[j * 32 : (j + 1) * 32, 128:]
            tile = wloc[j, :, :, cols].reshape(32, 128)
            ones.append(zr * tile)
            twos.append(zi * tile)
            gloc[j, :, :, cols] = (zr * use_ref[0, j] + zi * use_ref[1, j]).reshape(4, 8, 128)
        return first + jnp.concatenate(ones, axis=0), second + jnp.concatenate(twos, axis=0)

    sums = (jnp.zeros((128, 128), F32),) * 2
    for pair in range(16):
        sums = adjoint(pair, sums)
    both = jnp.concatenate(sums, axis=1)
    send_back(right2(both, fold[...]), 1, scale_cells)
    for part in range(4):
        for k in (2, 1, 3):
            to = (s + k) % 4
            push(gloc.at[to, part], grecv.at[part, k - 1], 14, 16 + part, (to, gx, h))
    middle_inverse(1)

    for part in range(4):
        arrived(grecv.at[part], 16 + part)
        gsum[part] = (gloc[s, part] + grecv[part, 0]) + (grecv[part, 1] + grecv[part, 2])
        own = jnp.logical_and(on_self, h % 4 == part)
        target = gspec.at[:, weight_cols(yp)]
        pl.when(own)(lambda: keep(gsum.at[part], target, 15))
        pl.when(jnp.logical_not(own))(lambda: push(gsum.at[part], target, 15, 15, owner(part)))

    def finish(c, half, value):
        grad[c, :, half] = value + local[c, :, half]

    depth_inverse(1, zl, finish)
    depth_inverse(1, 1 - zl, finish)
    grad_out = pltpu.make_async_copy(grad, gi_hbm, done_sem.at[0])
    grad_out.start()
    arrived(gspec, 15)
    spec_out = pltpu.make_async_copy(gspec, gs_hbm, done_sem.at[1])
    spec_out.start()

    for n in range(2):
        sent(out1.at[n, pl.ds(0, 7)], 6 * n)
        sent(out2.at[n, pl.ds(0, 15)], 6 * n + 2)
        sent(out5.at[n, pl.ds(0, 15)], 6 * n + 3)
        sent(out6.at[n, pl.ds(0, 7)], 6 * n + 4)
    sent(wloc.at[pl.ds(0, 3)], 13)
    sent(gloc.at[pl.ds(0, 3)], 14)
    sent(weight.at[:, pl.ds(0, 6144)], 12)
    sent(gsum.at[pl.ds(0, 3)], 15)

    @pl.when(jnp.logical_not(on_self))
    def _():
        sent(weight.at[:, pl.ds(0, 2048)], 12)
        sent(gsum.at[0], 15)

    grad_out.wait()
    spec_out.wait()


def hand_over(grad, gspec, grad_out, gspec_out, held, held_spec, in_sem, out_sem):
    first = [pltpu.make_async_copy(gspec, held_spec, in_sem.at[8])]
    second = [pltpu.make_async_copy(held_spec, gspec_out, out_sem.at[8])]
    for k in range(8):
        part = pl.ds(k * 4, 4)
        first.append(pltpu.make_async_copy(grad.at[part], held.at[part], in_sem.at[k]))
        second.append(pltpu.make_async_copy(held.at[part], grad_out.at[part], out_sem.at[k]))
    for copy in first:
        copy.start()
    for k in range(9):
        first[k].wait()
        second[k].start()
    for copy in second:
        copy.wait()


def body(field, cotangent, spectral_weight, pointwise_weight, bias):
    shape = (C, 8, 2, 8, NZ)
    big = (2, 8, 2, 8, 8, 128)
    ring = (2, 16, 16, 128)
    rows = (4, 4, 8, 2048)
    any_spec = pl.BlockSpec(memory_space=pl.ANY)
    grad_input, grad_spectral = pl.pallas_call(
        kernel,
        out_shape=(
            jax.ShapeDtypeStruct(shape, F32),
            jax.ShapeDtypeStruct(spectral_weight.shape, F32),
        ),
        in_specs=[any_spec] * 3
        + [pl.BlockSpec(memory_space=pltpu.VMEM), pl.BlockSpec(memory_space=pltpu.SMEM)]
        + [any_spec] * len(TABLES),
        out_specs=(any_spec, any_spec),
        scratch_shapes=[pltpu.VMEM(t.shape, BF16) for t in TABLES]
        + [
            pltpu.VMEM(shape, F32),
            pltpu.VMEM(shape, F32),
            pltpu.VMEM((8, 8192), F32),
            pltpu.VMEM(shape, F32),
            pltpu.VMEM(shape, F32),
            pltpu.VMEM(shape, F32),
            pltpu.VMEM((8, 8192), F32),
            pltpu.VMEM(rows, F32),
            pltpu.VMEM(rows, F32),
            pltpu.VMEM((4, 3, 8, 2048), F32),
            pltpu.VMEM(rows[1:], F32),
            pltpu.VMEM((2, 256, 256), BF16),
            pltpu.VMEM((2, 4, 32, 128), F32),
            pltpu.VMEM(big, F32),
            pltpu.VMEM(big, F32),
            pltpu.VMEM(ring, F32),
            pltpu.VMEM(ring, F32),
            pltpu.VMEM(ring, F32),
            pltpu.VMEM(ring, F32),
            pltpu.VMEM(big, F32),
            pltpu.VMEM(big, F32),
            pltpu.SemaphoreType.DMA((3,)),
            pltpu.SemaphoreType.DMA((len(TABLES),)),
            pltpu.SemaphoreType.DMA((2,)),
            pltpu.SemaphoreType.DMA((16,)),
            pltpu.SemaphoreType.DMA((24,)),
        ],
        compiler_params=pltpu.CompilerParams(
            has_side_effects=True, collective_id=0, vmem_limit_bytes=63 * 1024 * 1024
        ),
        name="fno_backward",
    )(
        field.reshape(shape),
        cotangent.reshape(shape),
        spectral_weight,
        pointwise_weight,
        bias,
        *[jnp.asarray(t) for t in TABLES],
    )
    grad_input, grad_spectral = pl.pallas_call(
        hand_over,
        out_shape=(
            jax.ShapeDtypeStruct(shape, F32),
            jax.ShapeDtypeStruct(spectral_weight.shape, F32),
        ),
        in_specs=[any_spec] * 2,
        out_specs=(any_spec, any_spec),
        scratch_shapes=[
            pltpu.VMEM(shape, F32),
            pltpu.VMEM(spectral_weight.shape, F32),
            pltpu.SemaphoreType.DMA((9,)),
            pltpu.SemaphoreType.DMA((9,)),
        ],
        compiler_params=pltpu.CompilerParams(vmem_limit_bytes=63 * 1024 * 1024),
        name="hand_over",
    )(grad_input, grad_spectral)
    return grad_input.reshape(field.shape), grad_spectral


def solution(mesh):
    placed = (
        P("dp", None, "gx", "gy", None),
        P("dp", None, "gx", "gy", None),
        P(("gx", "gy"), "dp"),
        P(),
        P(),
    )
    return jax.shard_map(
        body,
        mesh=mesh,
        in_specs=placed,
        out_specs=(P("dp", None, "gx", "gy", None), P(("gx", "gy"), "dp")),
        check_vma=False,
    )
```

```python
import math

import jax
import jax.numpy as jnp
import numpy as np
from jax import lax
from jax.experimental import pallas as pl
from jax.experimental.pallas import tpu as pltpu
from jax.sharding import PartitionSpec as P

C = 32
MX = 16
MY = 32
MZ = 16
NX = 64
NY = 128
NZ = 128

F32 = jnp.float32
BF16 = jnp.bfloat16
MESH = pl.DeviceIdType.MESH

KX = np.array([4 * ((d // 2) % 4) + 2 * (d % 2) + d // 8 for d in range(16)])

FAR_FIRST = (8, 7, 9, 6, 10, 5, 11, 4, 12, 3, 13, 2, 14, 1, 15)


def cos_sin(count, freqs):
    turns = np.mod(np.arange(count)[:, None] * freqs[None, :], count)
    theta = turns * (2.0 * math.pi / count)
    return np.cos(theta), np.sin(theta)


def halves(table):
    table = table.astype(np.float32)
    high = table.astype(jnp.bfloat16)
    low = (table - high.astype(np.float32)).astype(jnp.bfloat16)
    return [high, low]


def tables():
    eye8 = np.eye(8)
    cz, sz = cos_sin(NZ, np.arange(MZ))
    ztable = np.stack([cz, -sz], -1)
    cx, sx = cos_sin(NX, KX - MX // 2)
    cy, sy = cos_sin(NY, np.arange(MY) - MY // 2)

    def forward(c, s):
        return np.stack([np.stack([c, -s], -1), np.stack([s, c], -1)], -2)

    def inverse(c, s):
        return np.stack([np.stack([c, s], -1), np.stack([-s, c], -1)], -2)

    z_fwd = np.einsum("zjyr,cd->czyrjd", ztable.reshape(NZ, 4, 4, 2), np.eye(4)).reshape(4 * NZ, 128)
    fx = forward(cx, sx).reshape(8, 8, 16, 2, 2)
    fx = fx.reshape(4, 2, 8, 16, 2, 2)
    x_fwd = np.einsum("gzxdrq,yw->zdqygrxw", fx, eye8).reshape(2, 256, 512)
    ix = inverse(cx, sx).reshape(8, 8, 16, 2, 2)
    ix = ix.reshape(4, 2, 8, 16, 2, 2)
    x_inv = np.einsum("gzxdqr,yw->zgrxydqw", ix, eye8).reshape(8, 128, 256)
    fy = forward(cy, sy).reshape(16, 8, MY, 2, 2)
    y_fwd = np.einsum("dyjqp->pjdqy", fy).reshape(64, 256)
    iy = inverse(cy, sy).reshape(16, 8, MY, 2, 2)
    y_inv = np.einsum("dyjpr->drypj", iy).reshape(256, 64)

    use = np.zeros((128, 2, 2, C, 2), np.float32)
    for i in range(C):
        use[i, 0, :, i, 0] = 1.0
        use[C + i, 0, :, i, 1] = -1.0
        use[C + i, 1, :, i, 0] = 1.0
        use[i, 1, :, i, 1] = 1.0
    spread = np.zeros((128, 16, 2, 2, C, 2), np.float32)
    for b in range(2):
        for o in range(C):
            spread[b * C + o, o // 2, b, o % 2] = 1.0
    spread = spread.reshape(128, 4096)
    fold = np.zeros((2, 2, C, 2, 128), np.float32)
    for i in range(C):
        fold[0, :, i, 0, i] = 1.0
        fold[1, :, i, 1, i] = 1.0
        fold[1, :, i, 0, C + i] = 1.0
        fold[0, :, i, 1, C + i] = -1.0
    pack = np.zeros((2, 8, 4, 4, 4, 128), np.float32)
    for p in range(2):
        for j in range(4):
            for c in range(C):
                pack[p, c // 4, j, c % 4, j, p * C + c] = 1.0
    pack = pack.reshape(256, 512)
    rows8 = np.repeat(np.eye(C), 8, axis=0)
    out = []
    high, low = halves(z_fwd)
    out.append(np.concatenate([high, low], axis=1))
    out.append(np.ascontiguousarray(np.concatenate([high, high], axis=1).T))
    out.append(np.ascontiguousarray(low.T))
    for t in (x_fwd, y_fwd, y_inv, x_inv):
        out.append(np.concatenate(halves(t), axis=-2))
    out += [
        t.astype(jnp.bfloat16)
        for t in (
            use.reshape(128, 256),
            spread,
            np.ascontiguousarray(spread.T),
            fold.reshape(256, 128),
            rows8,
            pack,
            np.ascontiguousarray(pack.T),
        )
    ]
    return out


TABLES = tables()


def gelu_slope(values):
    normal_cdf = 0.5 * (1.0 + lax.erf(values * math.sqrt(0.5)))
    return normal_cdf + values * jnp.exp(-0.5 * values * values) * (1.0 / math.sqrt(2.0 * math.pi))


def split(x):
    high = x.astype(BF16)
    return high, (x - high.astype(F32)).astype(BF16)


def dot(a, b):
    return jnp.dot(a, b, preferred_element_type=F32)


def left3(table, x):
    half = table.shape[0] // 2
    y = dot(table, jnp.concatenate(split(x), axis=1))
    return y[:half, :128] + (y[half:, :128] + y[:half, 128:])


def right2(x, table):
    half = x.shape[0]
    y = dot(jnp.concatenate(split(x), axis=0), table)
    return y[:half] + y[half:]


def lanes_of(rows):
    return lax.broadcasted_iota(jnp.int32, (rows, 128), 1)


def roll(x, shift):
    shift = shift % 128
    return pltpu.roll(x, shift, axis=1) if shift else x


def swap_groups(blocks):
    lane = lanes_of(64)
    for bit in (4, 2, 1):
        width = 16 * bit
        low = lane % (2 * width) < width
        out = [None] * 8
        for a in range(8):
            if a & bit:
                continue
            first, second = blocks[a], blocks[a + bit]
            if bit == 4:
                moved = roll(jnp.where(low, second, first), 64)
                out[a] = jnp.where(low, first, moved)
                out[a + bit] = jnp.where(low, moved, second)
            else:
                out[a] = jnp.where(low, first, roll(second, width))
                out[a + bit] = jnp.where(low, roll(first, -width), second)
        blocks = out
    return blocks


def kernel(
    field_hbm,
    cot_hbm,
    weight_hbm,
    point_ref,
    bias_ref,
    *rest,
):
    n_tab = len(TABLES)
    tab_hbm = rest[:n_tab]
    gi_hbm, gs_hbm = rest[n_tab : n_tab + 2]
    scratch = rest[n_tab + 2 :]
    tab = scratch[:n_tab]
    (
        field,
        cot,
        weight,
        local,
        slope,
        grad,
        gspec,
        wloc,
        gloc,
        grecv,
        gsum,
        point_kron,
        use_ref,
        out1,
        recv1,
        out2,
        recv2,
        out5,
        recv5,
        out6,
        recv6,
        in_sem,
        tab_sem,
        done_sem,
        send_sem,
        recv_sem,
    ) = scratch[n_tab:]
    (zf, zi, zil, xf, yf, yi, xi, use, spread, gather, fold, rows8, pack, unpack) = tab

    s = lax.axis_index("dp")
    gx = lax.axis_index("gx")
    h = lax.axis_index("gy")
    yp = gx // 2
    zl = gx % 2
    place = 2 * h + zl
    on_self = yp == h % 4
    scale_cells = 1.0 / math.sqrt(NX * NY * NZ)
    scale_modes = 1.0 / math.sqrt(MX * MY * MZ)

    def mover(k):
        return (s, 2 * k + zl, (h // 4) * 4 + yp)

    def owner(k):
        return (s, 2 * (h % 4) + zl, (h // 4) * 4 + k)

    barrier = pltpu.get_barrier_semaphore()

    def hello(device):
        pl.semaphore_signal(barrier, inc=1, device_id=device, device_id_type=MESH)

    for k in FAR_FIRST:
        to = (place + k) % 16
        hello((s, 2 * yp + to % 2, to // 2))
    for k in range(1, 8):
        hello((s, (gx + k) % 8, h))
    for k in range(1, 4):
        hello(((s + k) % 4, gx, h))
        hello(mover((yp + k) % 4))
        hello(owner((h + k) % 4))

    @pl.when(jnp.logical_not(on_self))
    def _():
        hello(mover(yp))
        hello(owner(h % 4))

    def fetch(k):
        return pltpu.make_async_copy(tab_hbm[k], tab[k], tab_sem.at[k])

    inputs = [
        pltpu.make_async_copy(a, b, in_sem.at[k])
        for k, (a, b) in enumerate(((field_hbm, field), (weight_hbm, weight), (cot_hbm, cot)))
    ]
    fetch(0).start()
    inputs[0].start()
    inputs[1].start()
    for k in range(1, n_tab):
        fetch(k).start()
    inputs[2].start()

    def push(src, dst, out_sem, in_sem, device):
        pltpu.make_async_remote_copy(
            src_ref=src,
            dst_ref=dst,
            send_sem=send_sem.at[out_sem],
            recv_sem=recv_sem.at[in_sem],
            device_id=device,
            device_id_type=MESH,
        ).start()

    def keep(src, dst, in_sem):
        pltpu.make_async_copy(src, dst, recv_sem.at[in_sem]).start()

    def arrived(buffer, in_sem):
        pltpu.make_async_copy(buffer, buffer, recv_sem.at[in_sem]).wait()

    def sent(buffer, out_sem):
        pltpu.make_async_copy(buffer, buffer, send_sem.at[out_sem]).wait()

    def send_gx(src, dst, stage, to_zl, dy):
        to_yp = (yp + dy) % 4
        block = to_zl * 4 + to_yp
        push(src.at[block], dst.at[zl * 4 + yp], stage, stage + zl, (s, 2 * to_yp + to_zl, h))

    def keep_gx(src, dst, stage):
        block = zl * 4 + yp
        keep(src.at[block], dst.at[block], stage + zl)

    def over_ring(src, dst, stage):
        for k in FAR_FIRST:
            to = (place + k) % 16
            push(src.at[to], dst.at[place], stage, stage, (s, 2 * yp + to % 2, to // 2))
        keep(src.at[place], dst.at[place], stage)

    def depth_forward(grid, half, dst):
        rows = jnp.concatenate(
            [
                jnp.concatenate([grid[b * 4 + k, :, half].reshape(64, 128) for k in range(4)], axis=1)
                for b in range(8)
            ],
            axis=0,
        )
        high, low = split(rows)
        wide = dot(high, zf[...])
        total = wide[:, :128] + (wide[:, 128:] + dot(low, zf[:, :128]))
        for a, block in enumerate(swap_groups([total[b * 64 : (b + 1) * 64] for b in range(8)])):
            dst[half * 4 + a // 2, a % 2] = block.reshape(8, 8, 128)

    def send_half(n, half_is_own):
        half = zl if half_is_own else 1 - zl
        for dy in (2, 1, 3):
            send_gx(out1.at[n], recv1.at[n], 6 * n, half, dy)
        if half_is_own:
            keep_gx(out1.at[n], recv1.at[n], 6 * n)
        else:
            send_gx(out1.at[n], recv1.at[n], 6 * n, half, 0)

    def middle_forward(n, scale):
        total = None
        for half in (zl, 1 - zl):
            part = recv1.at[n, pl.ds(half * 4, 4)]
            arrived(part, 6 * n + half)
            term = left3(xf[half], part[...].reshape(512, 128))
            total = term if total is None else total + term
        out2[n] = total.reshape(16, 16, 128)
        over_ring(out2.at[n], recv2.at[n], 6 * n + 2)
        arrived(recv2.at[n], 6 * n + 2)
        v = left3(yf[...], recv2[n].reshape(256, 128)) * scale
        v = right2(jnp.concatenate([v[:32], v[32:]], axis=1), pack[...])
        return jnp.concatenate([v[:, j * 128 : (j + 1) * 128] for j in range(4)], axis=0)

    def send_back(rows, n, scale):
        flat = jnp.concatenate([rows[j * 32 : (j + 1) * 32] * scale for j in range(4)], axis=1)
        flat = right2(flat, unpack[...])
        planes = jnp.concatenate([flat[:, :128], flat[:, 128:]], axis=0)
        out5[n] = left3(yi[...], planes).reshape(16, 16, 128)
        over_ring(out5.at[n], recv5.at[n], 6 * n + 3)

    def middle_inverse(n):
        arrived(recv5.at[n], 6 * n + 3)
        rows = jnp.concatenate(split(recv5[n].reshape(256, 128)), axis=1)
        for half_is_own in (False, True):
            half = zl if half_is_own else 1 - zl
            for dy in (2, 1, 3, 0):
                block = half * 4 + (yp + dy) % 4
                value = dot(xi[block], rows)
                value = value[:128, :128] + (value[128:, :128] + value[:128, 128:])
                out6[n, block] = value.reshape(2, 8, 8, 128)
                if half_is_own and dy == 0:
                    keep_gx(out6.at[n], recv6.at[n], 6 * n + 4)
                else:
                    send_gx(out6.at[n], recv6.at[n], 6 * n + 4, half, dy)

    def depth_inverse(n, half, finish):
        arrived(recv6.at[n, pl.ds(half * 4, 4)], 6 * n + 4 + half)
        blocks = swap_groups([recv6[n, half * 4 + a // 2, a % 2].reshape(64, 128) for a in range(8)])
        high, low = split(jnp.concatenate(blocks, axis=0))
        both = jnp.concatenate([high, low], axis=1)
        for pair in range(2):
            cols = pl.ds(pair * 256, 256)
            value = dot(both, zi[:, cols]) + dot(high, zil[:, cols])
            for b in range(8):
                for k in range(2):
                    finish(
                        b * 4 + pair * 2 + k,
                        half,
                        value[b * 64 : (b + 1) * 64, k * 128 : (k + 1) * 128].reshape(8, 8, 128),
                    )

    def kron(transposed):
        same = lax.broadcasted_iota(jnp.int32, (256, 256), 0) % 8 == (
            lax.broadcasted_iota(jnp.int32, (256, 256), 1) % 8
        )
        dims = (((1,), (1 if transposed else 0,)), ((), ()))
        for k, half in enumerate(split(point_ref[...])):
            tall = lax.dot_general(rows8[...], half, dims, preferred_element_type=F32).astype(BF16)
            wide = lax.dot_general(
                tall, rows8[...], (((1,), (1,)), ((), ())), preferred_element_type=F32
            )
            point_kron[k] = jnp.where(same, wide, 0.0).astype(BF16)

    def pointwise(src, dst):
        def one(x, carry):
            block = jnp.concatenate([src[:, x, yh].reshape(256, 128) for yh in range(2)], axis=1)
            high, low = split(block)
            value = dot(point_kron[0], high) + (dot(point_kron[1], high) + dot(point_kron[0], low))
            for yh in range(2):
                dst[:, x, yh] = value[:, yh * 128 : (yh + 1) * 128].reshape(32, 8, 128)
            return carry

        lax.fori_loop(0, 8, one, 0)

    def weight_cols(k):
        return pl.ds(pl.multiple_of(k * 2048, 2048), 2048)

    def move_weights():
        inputs[1].wait()

        def one(k):
            push(weight.at[:, weight_cols(k)], wloc.at[s, h % 4], 12, 20 + h % 4, mover(k))

        for k in range(1, 4):
            one((yp + k) % 4)
        pl.when(on_self)(lambda: keep(weight.at[:, weight_cols(yp)], wloc.at[s, h % 4], 20 + h % 4))
        pl.when(jnp.logical_not(on_self))(lambda: one(yp))

    def spread_weights():
        for part in (h % 4, (h // 2 % 2) * 2 + 1 - h % 2, (1 - h // 2 % 2) * 2 + h % 2, 3 - h % 4):
            block = wloc.at[s, part]
            arrived(block, 20 + part)
            for k in (1, 3, 2):
                push(block, block, 13, 13, ((s + k) % 4, gx, h))

    def wait_weights():
        arrived(wloc.at[pl.ds(0, 3)], 13)

    fetch(0).wait()
    inputs[0].wait()
    depth_forward(field, 1 - zl, out1.at[0])
    pl.when(on_self)(lambda: pl.semaphore_wait(barrier, 31))
    pl.when(jnp.logical_not(on_self))(lambda: pl.semaphore_wait(barrier, 33))
    move_weights()
    send_half(0, False)
    depth_forward(field, zl, out1.at[0])
    send_half(0, True)
    spread_weights()
    for k in range(1, n_tab):
        fetch(k).wait()
    kron(False)
    pointwise(field, local)

    operands = right2(middle_forward(0, scale_cells), use[...])
    for b in range(2):
        use_ref[b] = operands[:, b * 128 : (b + 1) * 128].reshape(4, 32, 128)
    wait_weights()

    def mix(pair, total):
        cols = pl.ds(pair * 128, 128)
        tiles = [wloc[j, :, :, cols].reshape(32, 128) for j in range(4)]
        both = [
            jnp.concatenate([use_ref[b, j] * tiles[j] for j in range(4)], axis=0) for b in range(2)
        ]
        rows = pl.ds(pair * 256, 256)
        return total + right2(jnp.concatenate(both, axis=1), gather[rows])

    mixed = jnp.zeros((128, 128), F32)
    for pair in range(16):
        mixed = mix(pair, mixed)
    send_back(mixed, 0, scale_modes)
    middle_inverse(0)

    inputs[2].wait()

    def slope_of(c, half, value):
        pre = value + local[c, :, half] + bias_ref[c]
        slope[c, :, half] = cot[c, :, half] * gelu_slope(pre)

    for half_is_own in (True, False):
        half = zl if half_is_own else 1 - zl
        depth_inverse(0, half, slope_of)
        depth_forward(slope, half, out1.at[1])
        send_half(1, half_is_own)
    kron(True)
    pointwise(slope, local)

    spectra = jnp.concatenate(split(middle_forward(1, scale_modes)), axis=0)

    def adjoint(pair, carry):
        first, second = carry
        cols = pl.ds(pair * 256, 256)
        wide = dot(spectra, spread[:, cols])
        wide = wide[:128] + wide[128:]
        cols = pl.ds(pair * 128, 128)
        ones, twos = [], []
        for j in range(4):
            zr = wide[j * 32 : (j + 1) * 32, :128]
            zi = wide[j * 32 : (j + 1) * 32, 128:]
            tile = wloc[j, :, :, cols].reshape(32, 128)
            ones.append(zr * tile)
            twos.append(zi * tile)
            gloc[j, :, :, cols] = (zr * use_ref[0, j] + zi * use_ref[1, j]).reshape(4, 8, 128)
        return first + jnp.concatenate(ones, axis=0), second + jnp.concatenate(twos, axis=0)

    sums = (jnp.zeros((128, 128), F32),) * 2
    for pair in range(16):
        sums = adjoint(pair, sums)
    both = jnp.concatenate(sums, axis=1)
    send_back(right2(both, fold[...]), 1, scale_cells)
    for i in range(4):
        part = (yp + i) % 4
        for k in (2, 1, 3):
            to = (s + k) % 4
            push(gloc.at[to, part], grecv.at[part, k - 1], 14, 16 + i, (to, gx, h))
    middle_inverse(1)

    for i in range(4):
        part = (yp + i) % 4
        arrived(grecv.at[part], 16 + i)
        gsum[part] = (gloc[s, part] + grecv[part, 0]) + (grecv[part, 1] + grecv[part, 2])
        own = jnp.logical_and(on_self, h % 4 == part)
        target = gspec.at[:, weight_cols(yp)]
        pl.when(own)(lambda: keep(gsum.at[part], target, 15))
        pl.when(jnp.logical_not(own))(lambda: push(gsum.at[part], target, 15, 15, owner(part)))

    def finish(c, half, value):
        grad[c, :, half] = value + local[c, :, half]

    depth_inverse(1, zl, finish)
    depth_inverse(1, 1 - zl, finish)
    grad_out = pltpu.make_async_copy(grad, gi_hbm, done_sem.at[0])
    grad_out.start()
    arrived(gspec, 15)
    spec_out = pltpu.make_async_copy(gspec, gs_hbm, done_sem.at[1])
    spec_out.start()

    for n in range(2):
        sent(out1.at[n, pl.ds(0, 7)], 6 * n)
        sent(out2.at[n, pl.ds(0, 15)], 6 * n + 2)
        sent(out5.at[n, pl.ds(0, 15)], 6 * n + 3)
        sent(out6.at[n, pl.ds(0, 7)], 6 * n + 4)
    sent(wloc.at[pl.ds(0, 3)], 13)
    sent(gloc.at[pl.ds(0, 3)], 14)
    sent(weight.at[:, pl.ds(0, 6144)], 12)
    sent(gsum.at[pl.ds(0, 3)], 15)

    @pl.when(jnp.logical_not(on_self))
    def _():
        sent(weight.at[:, pl.ds(0, 2048)], 12)
        sent(gsum.at[0], 15)

    grad_out.wait()
    spec_out.wait()


def hand_over(grad, gspec, grad_out, gspec_out, held, held_spec, in_sem, out_sem):
    first = [pltpu.make_async_copy(gspec, held_spec, in_sem.at[8])]
    second = [pltpu.make_async_copy(held_spec, gspec_out, out_sem.at[8])]
    for k in range(8):
        part = pl.ds(k * 4, 4)
        first.append(pltpu.make_async_copy(grad.at[part], held.at[part], in_sem.at[k]))
        second.append(pltpu.make_async_copy(held.at[part], grad_out.at[part], out_sem.at[k]))
    for copy in first:
        copy.start()
    for k in range(9):
        first[k].wait()
        second[k].start()
    for copy in second:
        copy.wait()


def body(field, cotangent, spectral_weight, pointwise_weight, bias):
    shape = (C, 8, 2, 8, NZ)
    big = (2, 8, 2, 8, 8, 128)
    ring = (2, 16, 16, 128)
    rows = (4, 4, 8, 2048)
    any_spec = pl.BlockSpec(memory_space=pl.ANY)
    grad_input, grad_spectral = pl.pallas_call(
        kernel,
        out_shape=(
            jax.ShapeDtypeStruct(shape, F32),
            jax.ShapeDtypeStruct(spectral_weight.shape, F32),
        ),
        in_specs=[any_spec] * 3
        + [pl.BlockSpec(memory_space=pltpu.VMEM), pl.BlockSpec(memory_space=pltpu.SMEM)]
        + [any_spec] * len(TABLES),
        out_specs=(any_spec, any_spec),
        scratch_shapes=[pltpu.VMEM(t.shape, BF16) for t in TABLES]
        + [
            pltpu.VMEM(shape, F32),
            pltpu.VMEM(shape, F32),
            pltpu.VMEM((8, 8192), F32),
            pltpu.VMEM(shape, F32),
            pltpu.VMEM(shape, F32),
            pltpu.VMEM(shape, F32),
            pltpu.VMEM((8, 8192), F32),
            pltpu.VMEM(rows, F32),
            pltpu.VMEM(rows, F32),
            pltpu.VMEM((4, 3, 8, 2048), F32),
            pltpu.VMEM(rows[1:], F32),
            pltpu.VMEM((2, 256, 256), BF16),
            pltpu.VMEM((2, 4, 32, 128), F32),
            pltpu.VMEM(big, F32),
            pltpu.VMEM(big, F32),
            pltpu.VMEM(ring, F32),
            pltpu.VMEM(ring, F32),
            pltpu.VMEM(ring, F32),
            pltpu.VMEM(ring, F32),
            pltpu.VMEM(big, F32),
            pltpu.VMEM(big, F32),
            pltpu.SemaphoreType.DMA((3,)),
            pltpu.SemaphoreType.DMA((len(TABLES),)),
            pltpu.SemaphoreType.DMA((2,)),
            pltpu.SemaphoreType.DMA((16,)),
            pltpu.SemaphoreType.DMA((24,)),
        ],
        compiler_params=pltpu.CompilerParams(
            has_side_effects=True, collective_id=0, vmem_limit_bytes=63 * 1024 * 1024
        ),
        name="fno_backward",
    )(
        field.reshape(shape),
        cotangent.reshape(shape),
        spectral_weight,
        pointwise_weight,
        bias,
        *[jnp.asarray(t) for t in TABLES],
    )
    grad_input, grad_spectral = pl.pallas_call(
        hand_over,
        out_shape=(
            jax.ShapeDtypeStruct(shape, F32),
            jax.ShapeDtypeStruct(spectral_weight.shape, F32),
        ),
        in_specs=[any_spec] * 2,
        out_specs=(any_spec, any_spec),
        scratch_shapes=[
            pltpu.VMEM(shape, F32),
            pltpu.VMEM(spectral_weight.shape, F32),
            pltpu.SemaphoreType.DMA((9,)),
            pltpu.SemaphoreType.DMA((9,)),
        ],
        compiler_params=pltpu.CompilerParams(vmem_limit_bytes=63 * 1024 * 1024),
        name="hand_over",
    )(grad_input, grad_spectral)
    return grad_input.reshape(field.shape), grad_spectral


def solution(mesh):
    placed = (
        P("dp", None, "gx", "gy", None),
        P("dp", None, "gx", "gy", None),
        P(("gx", "gy"), "dp"),
        P(),
        P(),
    )
    return jax.shard_map(
        body,
        mesh=mesh,
        in_specs=placed,
        out_specs=(P("dp", None, "gx", "gy", None), P(("gx", "gy"), "dp")),
        check_vma=False,
    )
```

```python
import math

import jax
import jax.numpy as jnp
import numpy as np
from jax import lax
from jax.experimental import pallas as pl
from jax.experimental.pallas import tpu as pltpu
from jax.sharding import PartitionSpec as P

C = 32
MX = 16
MY = 32
MZ = 16
NX = 64
NY = 128
NZ = 128

F32 = jnp.float32
BF16 = jnp.bfloat16
MESH = pl.DeviceIdType.MESH

KX = np.array([4 * ((d // 2) % 4) + 2 * (d % 2) + d // 8 for d in range(16)])

FAR_FIRST = (8, 7, 9, 6, 10, 5, 11, 4, 12, 3, 13, 2, 14, 1, 15)


def cos_sin(count, freqs):
    turns = np.mod(np.arange(count)[:, None] * freqs[None, :], count)
    theta = turns * (2.0 * math.pi / count)
    return np.cos(theta), np.sin(theta)


def halves(table):
    table = table.astype(np.float32)
    high = table.astype(jnp.bfloat16)
    low = (table - high.astype(np.float32)).astype(jnp.bfloat16)
    return [high, low]


def tables():
    eye8 = np.eye(8)
    cz, sz = cos_sin(NZ, np.arange(MZ))
    ztable = np.stack([cz, -sz], -1)
    cx, sx = cos_sin(NX, KX - MX // 2)
    cy, sy = cos_sin(NY, np.arange(MY) - MY // 2)

    def forward(c, s):
        return np.stack([np.stack([c, -s], -1), np.stack([s, c], -1)], -2)

    def inverse(c, s):
        return np.stack([np.stack([c, s], -1), np.stack([-s, c], -1)], -2)

    z_fwd = np.einsum("zjyr,cd->czyrjd", ztable.reshape(NZ, 4, 4, 2), np.eye(4)).reshape(4 * NZ, 128)
    fx = forward(cx, sx).reshape(8, 8, 16, 2, 2)
    fx = fx.reshape(4, 2, 8, 16, 2, 2)
    x_fwd = np.einsum("gzxdrq,yw->zdqygrxw", fx, eye8).reshape(2, 256, 512)
    ix = inverse(cx, sx).reshape(8, 8, 16, 2, 2)
    ix = ix.reshape(4, 2, 8, 16, 2, 2)
    x_inv = np.einsum("gzxdqr,yw->zgrxydqw", ix, eye8).reshape(8, 128, 256)
    fy = forward(cy, sy).reshape(16, 8, MY, 2, 2)
    y_fwd = np.einsum("dyjqp->pjdqy", fy).reshape(64, 256)
    iy = inverse(cy, sy).reshape(16, 8, MY, 2, 2)
    y_inv = np.einsum("dyjpr->drypj", iy).reshape(256, 64)

    use = np.zeros((128, 2, 2, C, 2), np.float32)
    for i in range(C):
        use[i, 0, :, i, 0] = 1.0
        use[C + i, 0, :, i, 1] = -1.0
        use[C + i, 1, :, i, 0] = 1.0
        use[i, 1, :, i, 1] = 1.0
    spread = np.zeros((128, 16, 2, 2, C, 2), np.float32)
    for b in range(2):
        for o in range(C):
            spread[b * C + o, o // 2, b, o % 2] = 1.0
    spread = spread.reshape(128, 4096)
    fold = np.zeros((2, 2, C, 2, 128), np.float32)
    for i in range(C):
        fold[0, :, i, 0, i] = 1.0
        fold[1, :, i, 1, i] = 1.0
        fold[1, :, i, 0, C + i] = 1.0
        fold[0, :, i, 1, C + i] = -1.0
    pack = np.zeros((2, 8, 4, 4, 4, 128), np.float32)
    for p in range(2):
        for j in range(4):
            for c in range(C):
                pack[p, c // 4, j, c % 4, j, p * C + c] = 1.0
    pack = pack.reshape(256, 512)
    rows8 = np.repeat(np.eye(C), 8, axis=0)
    out = []
    high, low = halves(z_fwd)
    out.append(np.concatenate([high, low], axis=1))
    out.append(np.ascontiguousarray(np.concatenate([high, high], axis=1).T))
    out.append(np.ascontiguousarray(low.T))
    for t in (x_fwd, y_fwd, y_inv, x_inv):
        out.append(np.concatenate(halves(t), axis=-2))
    out += [
        t.astype(jnp.bfloat16)
        for t in (
            use.reshape(128, 256),
            spread,
            np.ascontiguousarray(spread.T),
            fold.reshape(256, 128),
            rows8,
            pack,
            np.ascontiguousarray(pack.T),
        )
    ]
    return out


TABLES = tables()


def gelu_slope(values):
    normal_cdf = 0.5 * (1.0 + lax.erf(values * math.sqrt(0.5)))
    return normal_cdf + values * jnp.exp(-0.5 * values * values) * (1.0 / math.sqrt(2.0 * math.pi))


def split(x):
    high = x.astype(BF16)
    return high, (x - high.astype(F32)).astype(BF16)


def dot(a, b):
    return jnp.dot(a, b, preferred_element_type=F32)


def left3(table, x):
    half = table.shape[0] // 2
    y = dot(table, jnp.concatenate(split(x), axis=1))
    return y[:half, :128] + (y[half:, :128] + y[:half, 128:])


def right2(x, table):
    half = x.shape[0]
    y = dot(jnp.concatenate(split(x), axis=0), table)
    return y[:half] + y[half:]


def lanes_of(rows):
    return lax.broadcasted_iota(jnp.int32, (rows, 128), 1)


def roll(x, shift):
    shift = shift % 128
    return pltpu.roll(x, shift, axis=1) if shift else x


def swap_groups(blocks):
    lane = lanes_of(64)
    for bit in (4, 2, 1):
        width = 16 * bit
        low = lane % (2 * width) < width
        out = [None] * 8
        for a in range(8):
            if a & bit:
                continue
            first, second = blocks[a], blocks[a + bit]
            if bit == 4:
                moved = roll(jnp.where(low, second, first), 64)
                out[a] = jnp.where(low, first, moved)
                out[a + bit] = jnp.where(low, moved, second)
            else:
                out[a] = jnp.where(low, first, roll(second, width))
                out[a + bit] = jnp.where(low, roll(first, -width), second)
        blocks = out
    return blocks


def kernel(
    field_hbm,
    cot_hbm,
    weight_hbm,
    point_ref,
    bias_ref,
    *rest,
):
    n_tab = len(TABLES)
    tab_hbm = rest[:n_tab]
    gi_hbm, gs_hbm = rest[n_tab : n_tab + 2]
    scratch = rest[n_tab + 2 :]
    tab = scratch[:n_tab]
    (
        field,
        cot,
        weight,
        local,
        slope,
        grad,
        gspec,
        wloc,
        gloc,
        grecv,
        gsum,
        point_kron,
        use_ref,
        out1,
        recv1,
        out2,
        recv2,
        out5,
        recv5,
        out6,
        recv6,
        in_sem,
        tab_sem,
        done_sem,
        send_sem,
        recv_sem,
    ) = scratch[n_tab:]
    (zf, zi, zil, xf, yf, yi, xi, use, spread, gather, fold, rows8, pack, unpack) = tab

    s = lax.axis_index("dp")
    gx = lax.axis_index("gx")
    h = lax.axis_index("gy")
    yp = gx // 2
    zl = gx % 2
    place = 2 * h + zl
    on_self = yp == h % 4
    scale_cells = 1.0 / math.sqrt(NX * NY * NZ)
    scale_modes = 1.0 / math.sqrt(MX * MY * MZ)

    def mover(k):
        return (s, 2 * k + zl, (h // 4) * 4 + yp)

    def owner(k):
        return (s, 2 * (h % 4) + zl, (h // 4) * 4 + k)

    barrier = pltpu.get_barrier_semaphore()

    def hello(device):
        pl.semaphore_signal(barrier, inc=1, device_id=device, device_id_type=MESH)

    for k in FAR_FIRST:
        to = (place + k) % 16
        hello((s, 2 * yp + to % 2, to // 2))
    for k in range(1, 8):
        hello((s, (gx + k) % 8, h))
    for k in range(1, 4):
        hello(((s + k) % 4, gx, h))
        hello(mover((yp + k) % 4))
        hello(owner((h + k) % 4))

    @pl.when(jnp.logical_not(on_self))
    def _():
        hello(mover(yp))
        hello(owner(h % 4))

    def fetch(k):
        return pltpu.make_async_copy(tab_hbm[k], tab[k], tab_sem.at[k])

    inputs = [
        pltpu.make_async_copy(a, b, in_sem.at[k])
        for k, (a, b) in enumerate(((field_hbm, field), (weight_hbm, weight), (cot_hbm, cot)))
    ]
    fetch(0).start()
    inputs[0].start()
    inputs[1].start()
    for k in range(1, n_tab):
        fetch(k).start()
    inputs[2].start()

    def push(src, dst, out_sem, in_sem, device):
        pltpu.make_async_remote_copy(
            src_ref=src,
            dst_ref=dst,
            send_sem=send_sem.at[out_sem],
            recv_sem=recv_sem.at[in_sem],
            device_id=device,
            device_id_type=MESH,
        ).start()

    def keep(src, dst, in_sem):
        pltpu.make_async_copy(src, dst, recv_sem.at[in_sem]).start()

    def arrived(buffer, in_sem):
        pltpu.make_async_copy(buffer, buffer, recv_sem.at[in_sem]).wait()

    def sent(buffer, out_sem):
        pltpu.make_async_copy(buffer, buffer, send_sem.at[out_sem]).wait()

    def send_gx(src, dst, stage, to_zl, dy):
        to_yp = (yp + dy) % 4
        block = to_zl * 4 + to_yp
        push(src.at[block], dst.at[zl * 4 + yp], stage, stage + zl, (s, 2 * to_yp + to_zl, h))

    def keep_gx(src, dst, stage):
        block = zl * 4 + yp
        keep(src.at[block], dst.at[block], stage + zl)

    def over_ring(src, dst, stage):
        for k in FAR_FIRST:
            to = (place + k) % 16
            push(src.at[to], dst.at[place], stage, stage, (s, 2 * yp + to % 2, to // 2))
        keep(src.at[place], dst.at[place], stage)

    def depth_forward(grid, half, dst):
        rows = jnp.concatenate(
            [
                jnp.concatenate([grid[b * 4 + k, :, half].reshape(64, 128) for k in range(4)], axis=1)
                for b in range(8)
            ],
            axis=0,
        )
        high, low = split(rows)
        wide = dot(high, zf[...])
        total = wide[:, :128] + (wide[:, 128:] + dot(low, zf[:, :128]))
        for a, block in enumerate(swap_groups([total[b * 64 : (b + 1) * 64] for b in range(8)])):
            dst[half * 4 + a // 2, a % 2] = block.reshape(8, 8, 128)

    def send_half(n, half_is_own):
        half = zl if half_is_own else 1 - zl
        for dy in (2, 1, 3):
            send_gx(out1.at[n], recv1.at[n], 6 * n, half, dy)
        if half_is_own:
            keep_gx(out1.at[n], recv1.at[n], 6 * n)
        else:
            send_gx(out1.at[n], recv1.at[n], 6 * n, half, 0)

    def middle_forward(n, scale):
        total = None
        for half in (zl, 1 - zl):
            part = recv1.at[n, pl.ds(half * 4, 4)]
            arrived(part, 6 * n + half)
            term = left3(xf[half], part[...].reshape(512, 128))
            total = term if total is None else total + term
        out2[n] = total.reshape(16, 16, 128)
        over_ring(out2.at[n], recv2.at[n], 6 * n + 2)
        arrived(recv2.at[n], 6 * n + 2)
        v = left3(yf[...], recv2[n].reshape(256, 128)) * scale
        v = right2(jnp.concatenate([v[:32], v[32:]], axis=1), pack[...])
        return jnp.concatenate([v[:, j * 128 : (j + 1) * 128] for j in range(4)], axis=0)

    def send_back(rows, n, scale):
        flat = jnp.concatenate([rows[j * 32 : (j + 1) * 32] * scale for j in range(4)], axis=1)
        flat = right2(flat, unpack[...])
        planes = jnp.concatenate([flat[:, :128], flat[:, 128:]], axis=0)
        out5[n] = left3(yi[...], planes).reshape(16, 16, 128)
        over_ring(out5.at[n], recv5.at[n], 6 * n + 3)

    def middle_inverse(n):
        arrived(recv5.at[n], 6 * n + 3)
        rows = jnp.concatenate(split(recv5[n].reshape(256, 128)), axis=1)
        for half_is_own in (False, True):
            half = zl if half_is_own else 1 - zl
            for dy in (2, 1, 3, 0):
                block = half * 4 + (yp + dy) % 4
                value = dot(xi[block], rows)
                value = value[:128, :128] + (value[128:, :128] + value[:128, 128:])
                out6[n, block] = value.reshape(2, 8, 8, 128)
                if half_is_own and dy == 0:
                    keep_gx(out6.at[n], recv6.at[n], 6 * n + 4)
                else:
                    send_gx(out6.at[n], recv6.at[n], 6 * n + 4, half, dy)

    def depth_inverse(n, half, finish):
        arrived(recv6.at[n, pl.ds(half * 4, 4)], 6 * n + 4 + half)
        blocks = swap_groups([recv6[n, half * 4 + a // 2, a % 2].reshape(64, 128) for a in range(8)])
        high, low = split(jnp.concatenate(blocks, axis=0))
        both = jnp.concatenate([high, low], axis=1)
        for pair in range(2):
            cols = pl.ds(pair * 256, 256)
            value = dot(both, zi[:, cols]) + dot(high, zil[:, cols])
            for b in range(8):
                for k in range(2):
                    finish(
                        b * 4 + pair * 2 + k,
                        half,
                        value[b * 64 : (b + 1) * 64, k * 128 : (k + 1) * 128].reshape(8, 8, 128),
                    )

    def kron(transposed):
        same = lax.broadcasted_iota(jnp.int32, (256, 256), 0) % 8 == (
            lax.broadcasted_iota(jnp.int32, (256, 256), 1) % 8
        )
        dims = (((1,), (1 if transposed else 0,)), ((), ()))
        for k, half in enumerate(split(point_ref[...])):
            tall = lax.dot_general(rows8[...], half, dims, preferred_element_type=F32).astype(BF16)
            wide = lax.dot_general(
                tall, rows8[...], (((1,), (1,)), ((), ())), preferred_element_type=F32
            )
            point_kron[k] = jnp.where(same, wide, 0.0).astype(BF16)

    def pointwise(src, dst, first, last):
        def one(x, carry):
            block = jnp.concatenate([src[:, x, yh].reshape(256, 128) for yh in range(2)], axis=1)
            high, low = split(block)
            value = dot(point_kron[0], high) + (dot(point_kron[1], high) + dot(point_kron[0], low))
            for yh in range(2):
                dst[:, x, yh] = value[:, yh * 128 : (yh + 1) * 128].reshape(32, 8, 128)
            return carry

        lax.fori_loop(first, last, one, 0)

    def weight_cols(k):
        return pl.ds(pl.multiple_of(k * 2048, 2048), 2048)

    def move_weights():
        inputs[1].wait()

        def one(k):
            push(weight.at[:, weight_cols(k)], wloc.at[s, h % 4], 12, 20 + h % 4, mover(k))

        for k in range(1, 4):
            one((yp + k) % 4)
        pl.when(on_self)(lambda: keep(weight.at[:, weight_cols(yp)], wloc.at[s, h % 4], 20 + h % 4))
        pl.when(jnp.logical_not(on_self))(lambda: one(yp))

    def spread_weights(parts):
        for part in parts:
            block = wloc.at[s, part]
            arrived(block, 20 + part)
            for k in (1, 3, 2):
                push(block, block, 13, 13, ((s + k) % 4, gx, h))

    def wait_weights():
        arrived(wloc.at[pl.ds(0, 3)], 13)

    fetch(0).wait()
    inputs[0].wait()
    depth_forward(field, 1 - zl, out1.at[0])
    pl.when(on_self)(lambda: pl.semaphore_wait(barrier, 31))
    pl.when(jnp.logical_not(on_self))(lambda: pl.semaphore_wait(barrier, 33))
    send_half(0, False)
    move_weights()
    depth_forward(field, zl, out1.at[0])
    send_half(0, True)
    for k in range(1, n_tab):
        fetch(k).wait()
    kron(False)
    spread_weights((h % 4, (h // 2 % 2) * 2 + 1 - h % 2))
    pointwise(field, local, 0, 4)
    spread_weights(((1 - h // 2 % 2) * 2 + h % 2, 3 - h % 4))
    pointwise(field, local, 4, 8)

    operands = right2(middle_forward(0, scale_cells), use[...])
    for b in range(2):
        use_ref[b] = operands[:, b * 128 : (b + 1) * 128].reshape(4, 32, 128)
    wait_weights()

    def mix(pair, total):
        cols = pl.ds(pair * 128, 128)
        tiles = [wloc[j, :, :, cols].reshape(32, 128) for j in range(4)]
        both = [
            jnp.concatenate([use_ref[b, j] * tiles[j] for j in range(4)], axis=0) for b in range(2)
        ]
        rows = pl.ds(pair * 256, 256)
        return total + right2(jnp.concatenate(both, axis=1), gather[rows])

    mixed = jnp.zeros((128, 128), F32)
    for pair in range(16):
        mixed = mix(pair, mixed)
    send_back(mixed, 0, scale_modes)
    middle_inverse(0)

    inputs[2].wait()

    def slope_of(c, half, value):
        pre = value + local[c, :, half] + bias_ref[c]
        slope[c, :, half] = cot[c, :, half] * gelu_slope(pre)

    for half_is_own in (True, False):
        half = zl if half_is_own else 1 - zl
        depth_inverse(0, half, slope_of)
        depth_forward(slope, half, out1.at[1])
        send_half(1, half_is_own)
    kron(True)
    pointwise(slope, local, 0, 8)

    spectra = jnp.concatenate(split(middle_forward(1, scale_modes)), axis=0)

    def adjoint(pair, carry):
        first, second = carry
        cols = pl.ds(pair * 256, 256)
        wide = dot(spectra, spread[:, cols])
        wide = wide[:128] + wide[128:]
        cols = pl.ds(pair * 128, 128)
        ones, twos = [], []
        for j in range(4):
            zr = wide[j * 32 : (j + 1) * 32, :128]
            zi = wide[j * 32 : (j + 1) * 32, 128:]
            tile = wloc[j, :, :, cols].reshape(32, 128)
            ones.append(zr * tile)
            twos.append(zi * tile)
            gloc[j, :, :, cols] = (zr * use_ref[0, j] + zi * use_ref[1, j]).reshape(4, 8, 128)
        return first + jnp.concatenate(ones, axis=0), second + jnp.concatenate(twos, axis=0)

    sums = (jnp.zeros((128, 128), F32),) * 2
    for pair in range(16):
        sums = adjoint(pair, sums)
    both = jnp.concatenate(sums, axis=1)
    send_back(right2(both, fold[...]), 1, scale_cells)
    for i in range(4):
        part = (yp + i) % 4
        for k in (1, 3, 2):
            to = (s + k) % 4
            push(gloc.at[to, part], grecv.at[part, k - 1], 14, 16 + i, (to, gx, h))
    middle_inverse(1)

    for i in range(4):
        part = (yp + i) % 4
        arrived(grecv.at[part], 16 + i)
        gsum[part] = (gloc[s, part] + grecv[part, 0]) + (grecv[part, 1] + grecv[part, 2])
        own = jnp.logical_and(on_self, h % 4 == part)
        target = gspec.at[:, weight_cols(yp)]
        pl.when(own)(lambda: keep(gsum.at[part], target, 15))
        pl.when(jnp.logical_not(own))(lambda: push(gsum.at[part], target, 15, 15, owner(part)))

    def finish(c, half, value):
        grad[c, :, half] = value + local[c, :, half]

    depth_inverse(1, zl, finish)
    depth_inverse(1, 1 - zl, finish)
    grad_out = pltpu.make_async_copy(grad, gi_hbm, done_sem.at[0])
    grad_out.start()
    arrived(gspec, 15)
    spec_out = pltpu.make_async_copy(gspec, gs_hbm, done_sem.at[1])
    spec_out.start()

    for n in range(2):
        sent(out1.at[n, pl.ds(0, 7)], 6 * n)
        sent(out2.at[n, pl.ds(0, 15)], 6 * n + 2)
        sent(out5.at[n, pl.ds(0, 15)], 6 * n + 3)
        sent(out6.at[n, pl.ds(0, 7)], 6 * n + 4)
    sent(wloc.at[pl.ds(0, 3)], 13)
    sent(gloc.at[pl.ds(0, 3)], 14)
    sent(weight.at[:, pl.ds(0, 6144)], 12)
    sent(gsum.at[pl.ds(0, 3)], 15)

    @pl.when(jnp.logical_not(on_self))
    def _():
        sent(weight.at[:, pl.ds(0, 2048)], 12)
        sent(gsum.at[0], 15)

    grad_out.wait()
    spec_out.wait()


def hand_over(grad, gspec, grad_out, gspec_out, held, held_spec, in_sem, out_sem):
    first = [pltpu.make_async_copy(gspec, held_spec, in_sem.at[8])]
    second = [pltpu.make_async_copy(held_spec, gspec_out, out_sem.at[8])]
    for k in range(8):
        part = pl.ds(k * 4, 4)
        first.append(pltpu.make_async_copy(grad.at[part], held.at[part], in_sem.at[k]))
        second.append(pltpu.make_async_copy(held.at[part], grad_out.at[part], out_sem.at[k]))
    for copy in first:
        copy.start()
    for k in range(9):
        first[k].wait()
        second[k].start()
    for copy in second:
        copy.wait()


def body(field, cotangent, spectral_weight, pointwise_weight, bias):
    shape = (C, 8, 2, 8, NZ)
    big = (2, 8, 2, 8, 8, 128)
    ring = (2, 16, 16, 128)
    rows = (4, 4, 8, 2048)
    any_spec = pl.BlockSpec(memory_space=pl.ANY)
    grad_input, grad_spectral = pl.pallas_call(
        kernel,
        out_shape=(
            jax.ShapeDtypeStruct(shape, F32),
            jax.ShapeDtypeStruct(spectral_weight.shape, F32),
        ),
        in_specs=[any_spec] * 3
        + [pl.BlockSpec(memory_space=pltpu.VMEM), pl.BlockSpec(memory_space=pltpu.SMEM)]
        + [any_spec] * len(TABLES),
        out_specs=(any_spec, any_spec),
        scratch_shapes=[pltpu.VMEM(t.shape, BF16) for t in TABLES]
        + [
            pltpu.VMEM(shape, F32),
            pltpu.VMEM(shape, F32),
            pltpu.VMEM((8, 8192), F32),
            pltpu.VMEM(shape, F32),
            pltpu.VMEM(shape, F32),
            pltpu.VMEM(shape, F32),
            pltpu.VMEM((8, 8192), F32),
            pltpu.VMEM(rows, F32),
            pltpu.VMEM(rows, F32),
            pltpu.VMEM((4, 3, 8, 2048), F32),
            pltpu.VMEM(rows[1:], F32),
            pltpu.VMEM((2, 256, 256), BF16),
            pltpu.VMEM((2, 4, 32, 128), F32),
            pltpu.VMEM(big, F32),
            pltpu.VMEM(big, F32),
            pltpu.VMEM(ring, F32),
            pltpu.VMEM(ring, F32),
            pltpu.VMEM(ring, F32),
            pltpu.VMEM(ring, F32),
            pltpu.VMEM(big, F32),
            pltpu.VMEM(big, F32),
            pltpu.SemaphoreType.DMA((3,)),
            pltpu.SemaphoreType.DMA((len(TABLES),)),
            pltpu.SemaphoreType.DMA((2,)),
            pltpu.SemaphoreType.DMA((16,)),
            pltpu.SemaphoreType.DMA((24,)),
        ],
        compiler_params=pltpu.CompilerParams(
            has_side_effects=True, collective_id=0, vmem_limit_bytes=63 * 1024 * 1024
        ),
        name="fno_backward",
    )(
        field.reshape(shape),
        cotangent.reshape(shape),
        spectral_weight,
        pointwise_weight,
        bias,
        *[jnp.asarray(t) for t in TABLES],
    )
    grad_input, grad_spectral = pl.pallas_call(
        hand_over,
        out_shape=(
            jax.ShapeDtypeStruct(shape, F32),
            jax.ShapeDtypeStruct(spectral_weight.shape, F32),
        ),
        in_specs=[any_spec] * 2,
        out_specs=(any_spec, any_spec),
        scratch_shapes=[
            pltpu.VMEM(shape, F32),
            pltpu.VMEM(spectral_weight.shape, F32),
            pltpu.SemaphoreType.DMA((9,)),
            pltpu.SemaphoreType.DMA((9,)),
        ],
        compiler_params=pltpu.CompilerParams(vmem_limit_bytes=63 * 1024 * 1024),
        name="hand_over",
    )(grad_input, grad_spectral)
    return grad_input.reshape(field.shape), grad_spectral


def solution(mesh):
    placed = (
        P("dp", None, "gx", "gy", None),
        P("dp", None, "gx", "gy", None),
        P(("gx", "gy"), "dp"),
        P(),
        P(),
    )
    return jax.shard_map(
        body,
        mesh=mesh,
        in_specs=placed,
        out_specs=(P("dp", None, "gx", "gy", None), P(("gx", "gy"), "dp")),
        check_vma=False,
    )
```
